256 devices in a mesh: pcol: 32 (over z, x), prow: 8 (over y, core).
Axes of the slice: x: 4, y: 4, z: 8, core: 2. Of those that a mesh axis runs over, the one named last changes fastest.
Arguments:
- matrix: float32 [8, 8, 128, 2, 32, 128], P(None, 'prow', None, None, 'pcol'), may hold values from -1 to 32, as said below
- node_width: int32 [64], replicated, may hold values from 32 to 128, as said below
- block_pattern: int32 [64, 64], replicated, may hold values from 0 to 1, as said below
- pivot_row_targets: int32 [4, 128], replicated, may hold values from 0 to 8191, as said below
- panel_order: int32 [4], replicated, may hold values from 0 to 63, as said below
Outputs:
- factored: float32 [8, 8, 128, 2, 32, 128], P(None, 'prow', None, None, 'pcol')
The draws below stay inside these ranges and needn't reach their ends.
Inputs may be any that keep to these rules, and one draw needn't show every extreme that they name: `panel_order`: 4 different supernode blocks. `node_width`: rows and columns of a block at or past its supernode's width are padding. `block_pattern`: every diagonal block is 1, and so is every block from which a panel takes a pivot row in the panel's block column. With p = panel_order[k]: pivot_row_targets[k, r] is p * 128 + r itself, or, only where r < node_width[p], a row within the width of a block that is no panel; all 512 entries are different. `matrix`: once a panel's rows are exchanged, and before any panel's update, each diagonal entry of its diagonal block is larger than the sum of the magnitudes of the other entries of that block in its row and in its column.
All inputs are finite; a program needn't handle non-finite values.
Results may differ from the reference program's by a relative error of at most 0.0001.
Values sent between devices are 32-bit elements; how exact they have to be, the bound alone decides.
No kernel may reach another device: no remote copies, remote signals or barrier semaphores. Data moves between devices by JAX's collectives and lax.ppermute only.
A program may use at most 64 MiB of HBM per device.

```python
import math
import jax
import jax.numpy as jnp
from jax import lax

B = 128
BC_DEV = 2
PANELS = 4
NB = 64
BR_DEV = 8
N_PCOL = 32
N_PROW = 8


def layout(key):
    drawn = jax.random.permutation(jax.random.fold_in(key, 101), NB).astype(jnp.int32)
    counter = jnp.arange(NB, dtype=jnp.int32)
    last_place = jnp.sum(jnp.where(drawn == NB - 1, counter, 0)).astype(jnp.int32)
    slot = jax.random.randint(jax.random.fold_in(key, 103), (), 0, PANELS).astype(jnp.int32)
    drawn = drawn.at[last_place].set(drawn[slot]).at[slot].set(NB - 1)
    elimination_step = drawn[:PANELS]
    donors = drawn[PANELS:2 * PANELS]
    widths = jax.random.randint(jax.random.fold_in(key, 102), (NB,), B // 4, B + 1).astype(jnp.int32)
    widths = widths.at[donors[0]].set(B).at[donors[1]].set(B // 4)
    positions = jnp.arange(B, dtype=jnp.int32)
    row_list = []
    for panel_step in range(PANELS):
        shuffle = jax.random.permutation(jax.random.fold_in(key, 110 + panel_step), B).astype(jnp.int32)
        coin_flip = jax.random.randint(jax.random.fold_in(key, 130 + panel_step), (B,), 0, 4) > 0
        swapped = coin_flip & (positions < widths[elimination_step[panel_step]]) & (shuffle < widths[donors[panel_step]])
        swapped = swapped & ~((elimination_step[panel_step] == NB - 1) & (positions == B - 1))
        row_list.append(jnp.where(swapped, donors[panel_step] * B + shuffle, elimination_step[panel_step] * B + positions))
    return (elimination_step, donors, widths, jnp.stack(row_list).astype(jnp.int32))


def draw_panel_order(key, part):
    elimination_step, donors, widths, pivots = layout(key)
    return elimination_step


def draw_node_width(key, part):
    elimination_step, donors, widths, pivots = layout(key)
    return widths


def draw_pivot_row_targets(key, part):
    elimination_step, donors, widths, pivots = layout(key)
    return pivots


def draw_block_pattern(key, part):
    elimination_step, donors, widths, pivots = layout(key)
    key = jax.random.fold_in(key, 7)
    density = jax.random.randint(jax.random.fold_in(key, 1), (NB,), 1, 5)
    draw_score = jax.random.randint(jax.random.fold_in(key, 2), (NB, NB), 0, 8)
    pattern = draw_score < density[None, :]
    pattern = pattern | jnp.eye(NB, dtype=bool)
    pattern = pattern.at[donors, elimination_step].set(True)
    return pattern.astype(jnp.int32)


def draw_matrix(key, part):
    elimination_step, donors, widths, pivots = layout(key)
    key = jax.random.fold_in(key, 5)
    full_shape = (BR_DEV, N_PROW, B, BC_DEV, N_PCOL, B)
    drawn_part = jax.random.uniform(jax.random.fold_in(key, 1), full_shape, jnp.float32, -1.0, 1.0)
    height = jnp.exp(jax.random.uniform(jax.random.fold_in(key, 2), full_shape, jnp.float32, math.log(16.0), math.log(32.0)))
    total = NB * B
    flat_pivots = pivots.reshape(-1)
    row_panel = jnp.full((total,), -1, jnp.int32).at[flat_pivots].set(jnp.repeat(jnp.arange(PANELS, dtype=jnp.int32), B))
    row_slot = jnp.zeros((total,), jnp.int32).at[flat_pivots].set(jnp.tile(jnp.arange(B, dtype=jnp.int32), PANELS))
    row_target = jnp.where(row_panel >= 0, elimination_step[jnp.maximum(row_panel, 0)], -1)
    row_index = jnp.arange(total, dtype=jnp.int32).reshape(BR_DEV, N_PROW, B)[:, :, :, None, None, None]
    col_index = jnp.arange(total, dtype=jnp.int32).reshape(BC_DEV, N_PCOL, B)[None, None, None, :, :, :]
    in_corner = row_target[row_index] == col_index // B
    on_pivot = in_corner & (row_slot[row_index] == col_index % B)
    entries = jnp.where(on_pivot, height, jnp.where(in_corner, drawn_part * 0.125, drawn_part))
    return entries.astype(jnp.float32)


def setup_inputs(seed: int = 0) -> dict:
    arg_keys = jax.random.split(jax.random.key(seed), 6)
    return {
        "matrix": draw_matrix(jax.random.fold_in(arg_keys[5], 71), 0),
        "node_width": draw_node_width(jax.random.fold_in(arg_keys[5], 71), 0),
        "block_pattern": draw_block_pattern(jax.random.fold_in(arg_keys[5], 71), 0),
        "pivot_row_targets": draw_pivot_row_targets(jax.random.fold_in(arg_keys[5], 71), 0),
        "panel_order": draw_panel_order(jax.random.fold_in(arg_keys[5], 71), 0),
    }


def reference(matrix, node_width, block_pattern, pivot_row_targets, panel_order):
    highest_pivot = lax.Precision.HIGHEST
    matrix_order = NB * B
    offsets = jnp.arange(B, dtype=jnp.int32)
    blocks = jnp.arange(NB, dtype=jnp.int32)
    live_rows = offsets[None, :] < node_width[:, None]
    kept_mask = (block_pattern[:, None, :, None] > 0) & live_rows[:, :, None, None] & live_rows[None, None, :, :]
    same_block = (blocks[:, None] == blocks[None, :])[:, None, :, None]
    diagonal = offsets[None, :, None, None] == offsets[None, None, None, :]
    padding = same_block & diagonal & (~live_rows)[:, :, None, None]
    working = jnp.where(kept_mask, matrix.reshape(NB, B, NB, B), 0.0)
    working = jnp.where(padding, 1.0, working).reshape(matrix_order, matrix_order)
    for panel_step in range(PANELS):
        panel_block = panel_order[panel_step].astype(jnp.int32)
        start = (panel_block * B).astype(jnp.int32)
        home = start + offsets
        targets = pivot_row_targets[panel_step].astype(jnp.int32)
        from_targets = working[targets]
        from_home = working[home]
        working = working.at[home].set(from_targets).at[targets].set(from_home)
        corner = lax.dynamic_slice(working, (start, start), (B, B))
        diagonal_inverse = jnp.linalg.inv(corner)
        earlier = panel_order[:panel_step]
        open_blocks = ~jnp.any(blocks[:, None] == earlier[None, :], axis=1) & (blocks != panel_block)
        open_rows = jnp.repeat(open_blocks, B)
        column_strip = lax.dynamic_slice_in_dim(working, start, B, 1)
        row_strip = lax.dynamic_slice_in_dim(working, start, B, 0)
        lower_factor = jnp.where(open_rows[:, None], jnp.dot(column_strip, diagonal_inverse, precision=highest_pivot), 0.0)
        upper_rows = jnp.where(open_rows[None, :], row_strip, 0.0)
        working = working - jnp.dot(lower_factor, upper_rows, precision=highest_pivot)
        column_new = jnp.where(open_rows[:, None], lower_factor, column_strip)
        working = lax.dynamic_update_slice_in_dim(working, column_new, start, 1)
    return working.reshape(matrix.shape)
```

```python
import functools

import jax
import jax.numpy as jnp
from jax import lax
from jax.experimental import pallas as pl
from jax.experimental.pallas import tpu as pltpu
from jax.sharding import Mesh, PartitionSpec as P

B = 128
PANELS = 4
S = PANELS * B
BR = 8
N_PROW = 8
N_PCOL = 32
NZ, NX, NY, NC = 8, 4, 4, 2
ROWS = BR * B
CHUNK = ROWS // N_PCOL
VMEM_LIMIT = 40 * 1024 * 1024
HIGHEST = lax.Precision.HIGHEST
F32 = jnp.float32
BF16 = jnp.bfloat16


def iota(shape, dim):
    return lax.broadcasted_iota(jnp.int32, shape, dim)


def dot_full(a, b):
    return jnp.dot(a, b, precision=HIGHEST, preferred_element_type=F32)


def dot_bf16(a, b):
    return jnp.dot(a, b, preferred_element_type=F32)


def split2(v):
    high = v.astype(BF16)
    low = (v - high.astype(F32)).astype(BF16)
    return high, low


def split3(v):
    high = v.astype(BF16)
    rest = v - high.astype(F32)
    middle = rest.astype(BF16)
    low = (rest - middle.astype(F32)).astype(BF16)
    return high, middle, low


def dot3(a, b):
    return dot_bf16(a[0], b[0]) + (dot_bf16(a[0], b[1]) + dot_bf16(a[1], b[0]))


def kept(value, here, row_width, col_width, same_block, row_start):
    rows = iota(value.shape, 0) + row_start
    cols = iota(value.shape, 1)
    value = jnp.where(here & (rows < row_width) & (cols < col_width), value, 0.0)
    return jnp.where(same_block & (rows == cols) & (rows >= row_width), 1.0, value)


def own_rows_kernel(pos, order, width, pattern, target_col, raw, pivots, homes, rows):
    r = pos[0]
    q = pos[1]
    for t in range(BR):
        block_row = t * N_PROW + r
        for s in range(2):
            block_col = s * N_PCOL + q
            rows[t * B : (t + 1) * B, s * B : (s + 1) * B] = kept(
                raw[pl.ds(t * 2 * B + s, B, stride=2), :],
                pattern[block_row, block_col] > 0,
                width[block_row],
                width[block_col],
                block_row == block_col,
                0,
            )
    gather_rows(target_col, rows, pivots, 2 * B)
    for k in range(PANELS):
        p = order[k]
        here = (p % N_PROW) == r
        block = rows[pl.ds(pl.multiple_of((p // N_PROW) * B, B), B), :]
        homes[k * B : (k + 1) * B, :] = jnp.where(here, block, 0.0)


def gather_rows(target_col, rows, out, columns):
    high, middle, low = split3(rows[...])
    for i in range(0, S, B):
        hot = iota((B, ROWS), 1) == target_col[i : i + B, :]
        hot = jnp.where(hot, 1.0, 0.0).astype(BF16)
        out[i : i + B, :] = dot_bf16(hot, high) + (dot_bf16(hot, middle) + dot_bf16(hot, low))


def select_kernel(pos, order, width, pattern, spread, out):
    r = pos[0]
    z = pos[2]
    x = pos[3]
    block_row = z * N_PROW + r
    for k in range(PANELS):
        p = order[k]
        source = p % N_PCOL
        value = jnp.where(
            p >= N_PCOL,
            spread[source, pl.ds(1, CHUNK, stride=2), :],
            spread[source, pl.ds(0, CHUNK, stride=2), :],
        )
        out[:, k * B : (k + 1) * B] = kept(
            value, pattern[block_row, p] > 0, width[block_row], width[p], block_row == p, x * CHUNK
        )


def natural_order(pos, parts, rows):
    z = pos[2]
    x = pos[3]
    for u in range(NX):
        for s in range(NZ):
            t = lax.rem(z - s + NZ, NZ)
            j = lax.rem(x - u + NX, NX)
            start = pl.multiple_of(t * B + j * CHUNK, CHUNK)
            rows[pl.ds(start, CHUNK), :] = parts[u][s]


def panel_rows_kernel(pos, order, target_col, part0, part1, part2, part3, mine, other, home_mine, home_other, rows, pivots, homes):
    r = pos[0]
    c = pos[4]
    natural_order(pos, (part0, part1, part2, part3), rows)
    gather_rows(target_col, rows, pivots, S)
    for k in range(PANELS):
        p = order[k]
        here = (p % N_PROW) == r
        block = rows[pl.ds(pl.multiple_of((p // N_PROW) * B, B), B), :]
        homes[k * B : (k + 1) * B, :] = jnp.where(here, block, 0.0)
    half = S // 2
    first = pl.multiple_of(c * half, half)
    second = pl.multiple_of((1 - c) * half, half)
    mine[...] = pivots[pl.ds(first, half), :]
    other[...] = pivots[pl.ds(second, half), :]
    home_mine[...] = homes[pl.ds(first, half), :]
    home_other[...] = homes[pl.ds(second, half), :]


def invert(corner, work, pivot_rows, out):
    row = iota((B, B), 0)
    col = iota((B, B), 1)
    eye = jnp.where(row == col, 1.0, 0.0)
    diagonal = jnp.where(row == col, corner, 0.0)
    by_col = 1.0 / jnp.sum(diagonal, axis=0, keepdims=True)
    by_row = 1.0 / jnp.sum(diagonal, axis=1, keepdims=True)
    residual = eye - corner * by_col
    approx = by_row * (eye + residual)

    def sweep(state):
        count, error, approx = state
        residual = eye - dot_full(corner, approx)
        return count + 1, jnp.max(jnp.abs(residual)), approx + dot_full(approx, residual)

    def again(state):
        count, error, approx = state
        return (count < 16) & jnp.logical_not(error < 1e-5)

    count, error, approx = lax.while_loop(again, sweep, (0, jnp.float32(1.0), approx))
    out[...] = approx

    @pl.when(jnp.logical_not(error < 1e-5))
    def _():
        work[:, :B] = corner
        work[:, B:] = eye
        row1 = iota((B, 1), 0)
        lane = iota((1, 2 * B), 1)

        def step(i, used):
            column = jnp.sum(jnp.where(iota((B, 2 * B), 1) == i, work[...], 0.0), axis=1, keepdims=True)
            size = jnp.where(used > 0.0, -1.0, jnp.abs(column))
            biggest = jnp.max(size)
            at = jnp.min(jnp.where(size == biggest, row1, B - 1))
            pivot_rows[i] = at
            line = jnp.sum(jnp.where(row1 == at, work[...], 0.0), axis=0, keepdims=True)
            line = line / jnp.sum(jnp.where(lane == i, line, 0.0))
            work[...] = jnp.where(row1 == at, line, work[...] - column * line)
            return jnp.where(row1 == at, 1.0, used)

        lax.fori_loop(0, B, step, jnp.zeros((B, 1), F32))

        def place(i, carry):
            line = jnp.sum(jnp.where(row1 == pivot_rows[i], work[:, B:], 0.0), axis=0, keepdims=True)
            out[...] = jnp.where(row1 == i, line, out[...])
            return carry

        lax.fori_loop(0, B, place, 0)


def corner_kernel(pos, a, b, other_a, other_b, own, factor, upper, inverses, work, pivot_rows):
    c = pos[4]
    half = S // 2
    first = pl.multiple_of(c * half, half)
    second = pl.multiple_of((1 - c) * half, half)
    factor[pl.ds(first, B), :] = a[...]
    factor[pl.ds(first + B, B), :] = b[...]
    factor[pl.ds(second, B), :] = other_a[...]
    factor[pl.ds(second + B, B), :] = other_b[...]
    upper[...] = own[...]
    for k in range(PANELS):
        here = slice(k * B, (k + 1) * B)
        later = slice((k + 1) * B, S)
        invert(factor[here, here], work, pivot_rows, inverses.at[k])
        if k + 1 < PANELS:
            lower = dot_full(factor[later, here], inverses[k])
            factor[later, here] = lower
            factor[later, later] = factor[later, later] - dot_full(lower, factor[here, later])
            upper[later, :] = upper[later, :] - dot_full(lower, upper[here, :])


def update_kernel(
    pos, order, width, pattern, target_row, raw, part0, part1, part2, part3,
    home_a, home_b, home_other_a, home_other_b, home_own, factor, upper, inverses,
    out, lower, final_homes,
):
    r = pos[0]
    q = pos[1]
    c = pos[4]
    half = S // 2
    natural_order(pos, (part0, part1, part2, part3), lower)
    first = pl.multiple_of(ROWS + c * half, half)
    second = pl.multiple_of(ROWS + (1 - c) * half, half)
    lower[pl.ds(first, B), :] = home_a[...]
    lower[pl.ds(first + B, B), :] = home_b[...]
    lower[pl.ds(second, B), :] = home_other_a[...]
    lower[pl.ds(second + B, B), :] = home_other_b[...]

    inverse_parts = [split2(inverses[k]) for k in range(PANELS)]
    factor_parts = [split2(factor[: k * B, k * B : (k + 1) * B]) for k in range(1, PANELS)]
    step_rows = 2 * B

    def solve(i, carry):
        here = pl.ds(pl.multiple_of(i * step_rows, step_rows), step_rows)
        for k in range(PANELS):
            value = lower[here, k * B : (k + 1) * B]
            if k:
                value = value - dot3(split2(lower[here, : k * B]), factor_parts[k - 1])
            lower[here, k * B : (k + 1) * B] = dot3(split2(value), inverse_parts[k])
        return carry

    lax.fori_loop(0, (ROWS + S) // step_rows, solve, 0)

    upper_parts = split2(upper[...])
    panel_of = []
    for s in range(2):
        found = jnp.int32(-1)
        for k in range(PANELS):
            found = jnp.where(order[k] == s * N_PCOL + q, k, found)
        panel_of.append(found)

    def finish(value, rows, s):
        at = pl.multiple_of(jnp.maximum(panel_of[s], 0) * B, B)
        return jnp.where(panel_of[s] >= 0, lower[rows, pl.ds(at, B)], value)

    for k in range(PANELS):
        rows = pl.ds(ROWS + k * B, B)
        here = slice(k * B, (k + 1) * B)
        value = home_own[here, :] - dot3(split2(lower[rows, :]), upper_parts)
        for s in range(2):
            final_homes[here, s * B : (s + 1) * B] = finish(value[:, s * B : (s + 1) * B], rows, s)
    home_parts = split3(final_homes[...])

    for t in range(BR):
        block_row = t * N_PROW + r
        rows = pl.ds(t * B, B)
        taken = dot3(split2(lower[rows, :]), upper_parts)
        hot = (iota((B, S), 0) + t * B) == target_row[...]
        hot = jnp.where(hot, 1.0, 0.0)
        replaced = jnp.max(hot, axis=1, keepdims=True) > 0.0
        hot = hot.astype(BF16)
        moved = dot_bf16(hot, home_parts[0]) + (dot_bf16(hot, home_parts[1]) + dot_bf16(hot, home_parts[2]))
        for s in range(2):
            block_col = s * N_PCOL + q
            cols = slice(s * B, (s + 1) * B)
            place = pl.ds(t * 2 * B + s, B, stride=2)
            value = kept(
                raw[place, :],
                pattern[block_row, block_col] > 0,
                width[block_row],
                width[block_col],
                block_row == block_col,
                0,
            )
            value = finish(value - taken[:, cols], rows, s)
            out[place, :] = jnp.where(replaced, moved[:, cols], value)
            for k in range(PANELS):

                @pl.when(order[k] == block_row)
                def _():
                    at = pl.multiple_of(jnp.maximum(panel_of[s], 0) * B, B)
                    here = slice(k * B, (k + 1) * B)
                    out[place, :] = jnp.where(panel_of[s] >= 0, factor[here, pl.ds(at, B)], upper[here, cols])


def call(kernel, smem, vmem, out_shapes, scratch):
    single = isinstance(out_shapes[0], int)
    shapes = [out_shapes] if single else list(out_shapes)
    in_specs = [pl.BlockSpec(memory_space=pltpu.SMEM)] * len(smem)
    in_specs += [pl.BlockSpec(memory_space=pltpu.VMEM)] * len(vmem)
    result = pl.pallas_call(
        kernel,
        out_shape=[jax.ShapeDtypeStruct(s, F32) for s in shapes],
        in_specs=in_specs,
        out_specs=[pl.BlockSpec(memory_space=pltpu.VMEM)] * len(shapes),
        scratch_shapes=scratch,
        compiler_params=pltpu.CompilerParams(vmem_limit_bytes=VMEM_LIMIT),
    )(*smem, *vmem)
    return result[0] if single else result


def shift(value, axis, size, by):
    return lax.ppermute(value, axis, [(i, (i + by) % size) for i in range(size)])


def merge_rows(mine, other):
    merged = mine + shift(other, "c", NC, 1)
    a = merged[:B]
    b = merged[B:]
    near = [(i, i ^ 1) for i in range(NY)]
    wrap = [(i, NY - 1 - i) for i in range(NY)]
    a = a + lax.ppermute(a, "y", near)
    b = b + lax.ppermute(b, "y", wrap)
    a = a + lax.ppermute(a, "y", wrap)
    b = b + lax.ppermute(b, "y", near)
    return a, b, shift(a, "c", NC, 1), shift(b, "c", NC, 1)


def body(matrix, node_width, block_pattern, pivot_row_targets, panel_order):
    z = lax.axis_index("z")
    x = lax.axis_index("x")
    c = lax.axis_index("c")
    r = lax.axis_index("y") * NC + c
    pos = jnp.stack([r, z * NX + x, z, x, c]).astype(jnp.int32)
    raw = matrix.reshape(ROWS * 2, B)
    targets = pivot_row_targets.reshape(-1)
    target_block = targets // B
    local = jnp.where(target_block % N_PROW == r, target_block // N_PROW * B + targets % B, -1)
    target_col = local.reshape(S, 1)
    target_row = local.reshape(1, S)

    spread = lax.all_to_all(raw.reshape(N_PCOL, CHUNK * 2, B), ("z", "x"), 0, 0)
    pivots, homes = call(
        own_rows_kernel,
        [pos, panel_order, node_width, block_pattern],
        [target_col, raw],
        [(S, 2 * B), (S, 2 * B)],
        [pltpu.VMEM((ROWS, 2 * B), F32)],
    )
    pivots, homes = lax.psum((pivots, homes), ("y", "c"))

    strip = call(
        select_kernel, [pos, panel_order, node_width, block_pattern], [spread], (CHUNK, S), []
    )
    strips = jnp.stack([strip] + [shift(strip, "z", NZ, s) for s in range(1, NZ)])
    parts = [strips] + [shift(strips, "x", NX, u) for u in range(1, NX)]

    mine, other, home_mine, home_other = call(
        panel_rows_kernel,
        [pos, panel_order],
        [target_col, *parts],
        [(S // 2, S)] * 4,
        [pltpu.VMEM((ROWS, S), F32), pltpu.VMEM((S, S), F32), pltpu.VMEM((S, S), F32)],
    )
    corner_rows = merge_rows(mine, other)
    home_rows = merge_rows(home_mine, home_other)
    factor, upper, inverses = call(
        corner_kernel,
        [pos],
        [*corner_rows, pivots],
        [(S, S), (S, 2 * B), (PANELS, B, B)],
        [pltpu.VMEM((B, 2 * B), F32), pltpu.SMEM((B,), jnp.int32)],
    )
    out = call(
        update_kernel,
        [pos, panel_order, node_width, block_pattern],
        [target_row, raw, *parts, *home_rows, homes, factor, upper, inverses],
        (ROWS * 2, B),
        [pltpu.VMEM((ROWS + S, S), F32), pltpu.VMEM((S, 2 * B), F32)],
    )
    return out.reshape(matrix.shape)


def solution(mesh):
    fine = Mesh(mesh.devices.reshape(NZ, NX, NY, NC), ("z", "x", "y", "c"))
    spec = P(None, ("y", "c"), None, None, ("z", "x"), None)
    return jax.shard_map(
        body,
        mesh=fine,
        in_specs=(spec, P(), P(), P(), P()),
        out_specs=spec,
        check_vma=False,
    )
```

```python
import jax
import jax.numpy as jnp
from jax import lax
from jax.experimental import pallas as pl
from jax.experimental.pallas import tpu as pltpu
from jax.sharding import Mesh, PartitionSpec as P

B = 128
PANELS = 4
S = PANELS * B
BR = 8
N_PROW = 8
N_PCOL = 32
NZ, NX, NY, NC = 8, 4, 4, 2
ROWS = BR * B
CHUNK = ROWS // N_PCOL
VMEM_LIMIT = 40 * 1024 * 1024
HIGHEST = lax.Precision.HIGHEST
F32 = jnp.float32
BF16 = jnp.bfloat16


def iota(shape, dim):
    return lax.broadcasted_iota(jnp.int32, shape, dim)


def dot_full(a, b):
    return jnp.dot(a, b, precision=HIGHEST, preferred_element_type=F32)


def dot_bf16(a, b):
    return jnp.dot(a, b, preferred_element_type=F32)


def split2(v):
    high = v.astype(BF16)
    low = (v - high.astype(F32)).astype(BF16)
    return high, low


def split3(v):
    high = v.astype(BF16)
    rest = v - high.astype(F32)
    middle = rest.astype(BF16)
    low = (rest - middle.astype(F32)).astype(BF16)
    return high, middle, low


def dot3(a, b):
    return dot_bf16(a[0], b[0]) + (dot_bf16(a[0], b[1]) + dot_bf16(a[1], b[0]))


def kept(value, here, row_width, col_width, same_block, row_start):
    rows = iota(value.shape, 0) + row_start
    cols = iota(value.shape, 1)
    value = jnp.where(here & (rows < row_width) & (cols < col_width), value, 0.0)
    return jnp.where(same_block & (rows == cols) & (rows >= row_width), 1.0, value)


def own_rows_kernel(pos, order, width, pattern, target_col, target_row, raw, keep, give, rows):
    r = pos[0]
    q = pos[1]
    c = pos[4]
    y = lax.div(r, NC)
    for t in range(BR):
        block_row = t * N_PROW + r
        for s in range(2):
            block_col = s * N_PCOL + q
            rows[t * B : (t + 1) * B, s * B : (s + 1) * B] = kept(
                raw[pl.ds(t * 2 * B + s, B, stride=2), :],
                pattern[block_row, block_col] > 0,
                width[block_row],
                width[block_col],
                block_row == block_col,
                0,
            )
    part = S // N_PROW
    high, middle, low = split3(rows[...])
    lane = iota((B, ROWS), 1)
    row_id = ((lane // B) * N_PROW + r) * B + lane % B
    for i in range(0, S, B):
        hot = jnp.where(row_id == target_col[i : i + B, :], 1.0, 0.0).astype(BF16)
        picked = dot_bf16(hot, high) + (dot_bf16(hot, middle) + dot_bf16(hot, low))
        place = lax.rem(i // B - y + NY, NY)
        keep[place, :part, :] = jnp.where(c == 0, picked[:part], picked[part:])
        give[place, :part, :] = jnp.where(c == 0, picked[part:], picked[:part])
    for k in range(PANELS):
        p = order[k]
        here = (p % N_PROW) == r
        block = rows[pl.ds(pl.multiple_of((p // N_PROW) * B, B), B), :]
        block = jnp.where(here, block, 0.0)
        place = lax.rem(k - y + NY, NY)
        keep[place, part:, :] = jnp.where(c == 0, block[:part], block[part:])
        give[place, part:, :] = jnp.where(c == 0, block[part:], block[:part])
    for t in range(BR):
        here = slice(t * B, (t + 1) * B)
        taken = is_target(target_row, B, (t * N_PROW + r) * B)
        rows[here, :] = jnp.where(taken, 0.0, rows[here, :])


def is_target(target_row, count, start):
    hot = jnp.where(iota((count, S), 0) + start == target_row[...], 1.0, 0.0)
    return jnp.max(hot, axis=1, keepdims=True) > 0.0


def add_kernel(keep, received, *sums):
    for u in range(NY):
        sums[u][...] = keep[u] + received[u]


def sum_kernel(part0, part1, part2, part3, total, packed):
    value = (part0[...] + part1[...]) + (part2[...] + part3[...])
    total[...] = value
    for s in range(2):
        for i in range(4):
            packed[pl.ds(s * 4 + i, N_PCOL, stride=8), :] = value[
                i * N_PCOL : (i + 1) * N_PCOL, s * B : (s + 1) * B
            ]


def select_few_kernel(order, spread, out):
    pieces = []
    for k in range(PANELS):
        p = order[k]
        block = spread[p % N_PCOL]
        pieces.append(jnp.where(p >= N_PCOL, block[4:], block[:4]))
    value = jnp.concatenate(pieces, axis=0)
    for j in range(N_PCOL):
        out[j] = value


def arrange_kernel(gathered, total, pivots, homes):
    for i in range(2):
        here = slice(i * N_PCOL, (i + 1) * N_PCOL)
        for k in range(PANELS):
            cols = slice(k * B, (k + 1) * B)
            pivots[here, cols] = gathered[pl.ds(k * 4 + i, N_PCOL, stride=16), :]
            homes[here, cols] = gathered[pl.ds(k * 4 + i + 2, N_PCOL, stride=16), :]
    half = S // N_PROW
    pivots[:, S:] = total[:half]
    homes[:, S:] = total[half:]


def select_kernel(pos, order, width, pattern, target_row, spread, out):
    r = pos[0]
    z = pos[2]
    x = pos[3]
    block_row = z * N_PROW + r
    taken = is_target(target_row, CHUNK, block_row * B + x * CHUNK)
    for k in range(PANELS):
        p = order[k]
        source = p % N_PCOL
        value = jnp.where(
            p >= N_PCOL,
            spread[source, pl.ds(1, CHUNK, stride=2), :],
            spread[source, pl.ds(0, CHUNK, stride=2), :],
        )
        value = kept(
            value, pattern[block_row, p] > 0, width[block_row], width[p], block_row == p, x * CHUNK
        )
        out[:, k * B : (k + 1) * B] = jnp.where(taken, 0.0, value)


def natural_order(pos, pairs, out, columns):
    c = pos[4]
    y = lax.div(pos[0], NC)
    part = S // N_PROW
    for u in range(NY):
        other_y = lax.rem(y - u + NY, NY)
        for i in range(NC):
            core = c if i == 0 else 1 - c
            start = pl.multiple_of((other_y * NC + core) * part, part)
            out[pl.ds(start, part), :] = pairs[u][i, :, columns]


def invert(corner, work, pivot_rows, out):
    row = iota((B, B), 0)
    col = iota((B, B), 1)
    eye = jnp.where(row == col, 1.0, 0.0)
    diagonal = jnp.where(row == col, corner, 0.0)
    by_col = 1.0 / jnp.sum(diagonal, axis=0, keepdims=True)
    by_row = 1.0 / jnp.sum(diagonal, axis=1, keepdims=True)
    residual = eye - corner * by_col
    approx = by_row * (eye + residual)

    def sweep(state):
        count, error, approx = state
        residual = eye - dot_full(corner, approx)
        return count + 1, jnp.max(jnp.abs(residual)), approx + dot_full(approx, residual)

    def again(state):
        count, error, approx = state
        return (count < 16) & jnp.logical_not(error < 1e-5)

    count, error, approx = lax.while_loop(again, sweep, (0, jnp.float32(1.0), approx))
    out[...] = approx

    @pl.when(jnp.logical_not(error < 1e-5))
    def _():
        work[:, :B] = corner
        work[:, B:] = eye
        row1 = iota((B, 1), 0)
        lane = iota((1, 2 * B), 1)

        def step(i, used):
            column = jnp.sum(jnp.where(iota((B, 2 * B), 1) == i, work[...], 0.0), axis=1, keepdims=True)
            size = jnp.where(used > 0.0, -1.0, jnp.abs(column))
            biggest = jnp.max(size)
            at = jnp.min(jnp.where(size == biggest, row1, B - 1))
            pivot_rows[i] = at
            line = jnp.sum(jnp.where(row1 == at, work[...], 0.0), axis=0, keepdims=True)
            line = line / jnp.sum(jnp.where(lane == i, line, 0.0))
            work[...] = jnp.where(row1 == at, line, work[...] - column * line)
            return jnp.where(row1 == at, 1.0, used)

        lax.fori_loop(0, B, step, jnp.zeros((B, 1), F32))

        def place(i, carry):
            line = jnp.sum(jnp.where(row1 == pivot_rows[i], work[:, B:], 0.0), axis=0, keepdims=True)
            out[...] = jnp.where(row1 == i, line, out[...])
            return carry

        lax.fori_loop(0, B, place, 0)


def corner_kernel(
    pos, pair0, pair1, pair2, pair3,
    factor, upper, solve_high, solve_low, upper_high, upper_low, inverses, work, solver, pivot_rows,
):
    pairs = (pair0, pair1, pair2, pair3)
    natural_order(pos, pairs, factor, slice(0, S))
    natural_order(pos, pairs, upper, slice(S, S + 2 * B))
    solver[...] = jnp.zeros((S, S), F32)
    for k in range(PANELS):
        here = slice(k * B, (k + 1) * B)
        later = slice((k + 1) * B, S)
        before = slice(0, k * B)
        invert(factor[here, here], work, pivot_rows, inverses)
        inverse = inverses[...]
        solver[here, here] = inverse
        if k + 1 < PANELS:
            lower = dot_full(factor[later, here], inverse)
            factor[later, here] = lower
            factor[later, later] = factor[later, later] - dot_full(lower, factor[here, later])
            upper[later, :] = upper[later, :] - dot_full(lower, upper[here, :])
        if k:
            solver[before, here] = -dot_full(dot_full(solver[before, before], factor[before, here]), inverse)
    high, low = split2(solver[...])
    solve_high[...] = high
    solve_low[...] = low
    high, low = split2(upper[...])
    upper_high[...] = high
    upper_low[...] = low


def update_kernel(
    pos, order, target_row, rows, part0, part1, part2, part3, pair0, pair1, pair2, pair3,
    factor, upper, solve_high, solve_low, upper_high, upper_low,
    out, lower, taken, home_rows, homes,
):
    r = pos[0]
    q = pos[1]
    z = pos[2]
    x = pos[3]
    half = S // 2
    upper_parts = (upper_high[...], upper_low[...])
    solve_first = (solve_high[:half, :half], solve_low[:half, :half])
    solve_second = (solve_high[:, half:], solve_low[:, half:])
    pairs = (pair0, pair1, pair2, pair3)
    natural_order(pos, pairs, home_rows, slice(0, S))
    natural_order(pos, pairs, homes, slice(S, S + 2 * B))

    panel_of = []
    for s in range(2):
        found = jnp.int32(-1)
        for k in range(PANELS):
            found = jnp.where(order[k] == s * N_PCOL + q, k, found)
        panel_of.append(found)

    def solve(value):
        high, low = split2(value)
        first = dot3((high[:, :half], low[:, :half]), solve_first)
        second = dot3((high, low), solve_second)
        value = jnp.concatenate([first, second], axis=1)
        return value, dot3(split2(value), upper_parts)

    for i in range(2):
        here = slice(i * half, (i + 1) * half)
        value, product = solve(home_rows[here, :])
        home_rows[here, :] = value
        homes[here, :] = homes[here, :] - product
    for u, part in enumerate((part0, part1, part2, part3)):
        value, product = solve(part[...].reshape(NZ * CHUNK, S))
        other_x = lax.rem(x - u + NX, NX)
        for i in range(NZ):
            t = lax.rem(z - i + NZ, NZ)
            place = pl.ds(pl.multiple_of(t * B + other_x * CHUNK, CHUNK), CHUNK)
            lower[place, :] = value[i * CHUNK : (i + 1) * CHUNK]
            taken[place, :] = product[i * CHUNK : (i + 1) * CHUNK]

    for s in range(2):
        cols = slice(s * B, (s + 1) * B)

        @pl.when(panel_of[s] >= 0)
        def _():
            at = pl.ds(pl.multiple_of(panel_of[s] * B, B), B)
            homes[:, cols] = home_rows[:, at]
            taken[:, cols] = -lower[:, at]

    home_parts = split3(homes[...])
    for t in range(BR):
        block_row = t * N_PROW + r
        here = slice(t * B, (t + 1) * B)
        hot = (iota((B, S), 0) + block_row * B) == target_row[...]
        hot = jnp.where(hot, 1.0, 0.0).astype(BF16)
        moved = dot_bf16(hot, home_parts[0]) + (dot_bf16(hot, home_parts[1]) + dot_bf16(hot, home_parts[2]))
        for s in range(2):
            cols = slice(s * B, (s + 1) * B)
            value = jnp.where(panel_of[s] >= 0, 0.0, rows[here, cols])
            out[pl.ds(t * 2 * B + s, B, stride=2), :] = (value - taken[here, cols]) + moved[:, cols]

    for k in range(PANELS):

        @pl.when(lax.rem(order[k], N_PROW) == r)
        def _():
            t = lax.div(order[k], N_PROW)
            here = slice(k * B, (k + 1) * B)
            for s in range(2):
                at = pl.multiple_of(jnp.maximum(panel_of[s], 0) * B, B)
                value = jnp.where(
                    panel_of[s] >= 0, factor[here, pl.ds(at, B)], upper[here, s * B : (s + 1) * B]
                )
                out[pl.ds(t * 2 * B + s, B, stride=2), :] = value


def call(kernel, smem, vmem, out_shapes, scratch):
    in_specs = [pl.BlockSpec(memory_space=pltpu.SMEM)] * len(smem)
    in_specs += [pl.BlockSpec(memory_space=pltpu.VMEM)] * len(vmem)
    return pl.pallas_call(
        kernel,
        out_shape=[jax.ShapeDtypeStruct(shape, kind) for kind, shape in out_shapes],
        in_specs=in_specs,
        out_specs=[pl.BlockSpec(memory_space=pltpu.VMEM)] * len(out_shapes),
        scratch_shapes=scratch,
        compiler_params=pltpu.CompilerParams(vmem_limit_bytes=VMEM_LIMIT),
    )(*smem, *vmem)


def shift(value, axis, size, by):
    return lax.ppermute(value, axis, [(i, (i + by) % size) for i in range(size)])


def gather_pairs(value):
    pair = jnp.stack([value, shift(value, "c", NC, 1)])
    return [pair] + [shift(pair, "y", NY, u) for u in range(1, NY)]


def body(matrix, node_width, block_pattern, pivot_row_targets, panel_order):
    z = lax.axis_index("z")
    x = lax.axis_index("x")
    c = lax.axis_index("c")
    r = lax.axis_index("y") * NC + c
    pos = jnp.stack([r, z * NX + x, z, x, c]).astype(jnp.int32)
    raw = matrix.reshape(ROWS * 2, B)
    target_col = pivot_row_targets.reshape(S, 1)
    target_row = pivot_row_targets.reshape(1, S)
    where = [pos, panel_order, node_width, block_pattern]
    part = S // N_PROW

    spread = lax.all_to_all(raw.reshape(N_PCOL, CHUNK * 2, B), ("z", "x"), 0, 0)
    keep, give, rows = call(
        own_rows_kernel,
        where,
        [target_col, target_row, raw],
        [(F32, (NY, 2 * part, 2 * B)), (F32, (NY, 2 * part, 2 * B)), (F32, (ROWS, 2 * B))],
        [],
    )
    sums = call(
        add_kernel, [], [keep, shift(give, "c", NC, 1)], [(F32, (2 * part, 2 * B))] * NY, []
    )
    sums = [sums[0]] + [shift(sums[u], "y", NY, u) for u in range(1, NY)]
    total, packed = call(
        sum_kernel, [], sums, [(F32, (2 * part, 2 * B)), (F32, (N_PCOL * 8, B))], []
    )
    spread, packed = lax.optimization_barrier((spread, packed))
    few = lax.all_to_all(packed.reshape(N_PCOL, 8, B), ("z", "x"), 0, 0)
    (few,) = call(select_few_kernel, [panel_order], [few], [(F32, (N_PCOL, 16, B))], [])
    few = lax.all_to_all(few, ("z", "x"), 0, 0)
    pivots, homes = call(
        arrange_kernel, [], [few.reshape(N_PCOL * 16, B), total], [(F32, (part, S + 2 * B))] * 2, []
    )
    pivots = gather_pairs(pivots)
    homes = gather_pairs(homes)
    solved = call(
        corner_kernel,
        [pos],
        pivots,
        [(F32, (S, S)), (F32, (S, 2 * B)), (BF16, (S, S)), (BF16, (S, S)), (BF16, (S, 2 * B)), (BF16, (S, 2 * B))],
        [
            pltpu.VMEM((B, B), F32),
            pltpu.VMEM((B, 2 * B), F32),
            pltpu.VMEM((S, S), F32),
            pltpu.SMEM((B,), jnp.int32),
        ],
    )

    (strip,) = call(select_kernel, where, [target_row, spread], [(F32, (CHUNK, S))], [])
    strips = jnp.stack([strip] + [shift(strip, "z", NZ, i) for i in range(1, NZ)])
    parts = [strips] + [shift(strips, "x", NX, u) for u in range(1, NX)]
    (out,) = call(
        update_kernel,
        [pos, panel_order],
        [target_row, rows, *parts, *homes, *solved],
        [(F32, (ROWS * 2, B))],
        [
            pltpu.VMEM((ROWS, S), F32),
            pltpu.VMEM((ROWS, 2 * B), F32),
            pltpu.VMEM((S, S), F32),
            pltpu.VMEM((S, 2 * B), F32),
        ],
    )
    return out.reshape(matrix.shape)


def solution(mesh):
    fine = Mesh(mesh.devices.reshape(NZ, NX, NY, NC), ("z", "x", "y", "c"))
    spec = P(None, ("y", "c"), None, None, ("z", "x"), None)
    return jax.shard_map(
        body,
        mesh=fine,
        in_specs=(spec, P(), P(), P(), P()),
        out_specs=spec,
        check_vma=False,
    )
```

```python
import jax
import jax.numpy as jnp
from jax import lax
from jax.experimental import pallas as pl
from jax.experimental.pallas import tpu as pltpu
from jax.sharding import Mesh, PartitionSpec as P

B = 128
PANELS = 4
S = PANELS * B
BR = 8
N_PROW = 8
N_PCOL = 32
NZ, NX, NY, NC = 8, 4, 4, 2
ROWS = BR * B
CHUNK = ROWS // N_PCOL
VMEM_LIMIT = 40 * 1024 * 1024
HIGHEST = lax.Precision.HIGHEST
F32 = jnp.float32
BF16 = jnp.bfloat16


def iota(shape, dim):
    return lax.broadcasted_iota(jnp.int32, shape, dim)


def dot_full(a, b):
    return jnp.dot(a, b, precision=HIGHEST, preferred_element_type=F32)


def dot_bf16(a, b):
    return jnp.dot(a, b, preferred_element_type=F32)


def split2(v):
    high = v.astype(BF16)
    low = (v - high.astype(F32)).astype(BF16)
    return high, low


def split3(v):
    high = v.astype(BF16)
    rest = v - high.astype(F32)
    middle = rest.astype(BF16)
    low = (rest - middle.astype(F32)).astype(BF16)
    return high, middle, low


def dot3(a, b):
    return dot_bf16(a[0], b[0]) + (dot_bf16(a[0], b[1]) + dot_bf16(a[1], b[0]))


def kept(value, here, row_width, col_width, same_block, row_start):
    rows = iota(value.shape, 0) + row_start
    cols = iota(value.shape, 1)
    value = jnp.where(here & (rows < row_width) & (cols < col_width), value, 0.0)
    return jnp.where(same_block & (rows == cols) & (rows >= row_width), 1.0, value)


def own_rows_kernel(pos, order, width, pattern, target_col, target_row, raw, keep, give, rows):
    r = pos[0]
    q = pos[1]
    c = pos[4]
    y = lax.div(r, NC)
    for t in range(BR):
        block_row = t * N_PROW + r
        for s in range(2):
            block_col = s * N_PCOL + q
            rows[t * B : (t + 1) * B, s * B : (s + 1) * B] = kept(
                raw[pl.ds(t * 2 * B + s, B, stride=2), :],
                pattern[block_row, block_col] > 0,
                width[block_row],
                width[block_col],
                block_row == block_col,
                0,
            )
    part = S // N_PROW
    high, middle, low = split3(rows[...])
    lane = iota((B, ROWS), 1)
    row_id = ((lane // B) * N_PROW + r) * B + lane % B
    for i in range(0, S, B):
        hot = jnp.where(row_id == target_col[i : i + B, :], 1.0, 0.0).astype(BF16)
        picked = dot_bf16(hot, high) + (dot_bf16(hot, middle) + dot_bf16(hot, low))
        place = lax.rem(i // B - y + NY, NY)
        keep[place, :part, :] = jnp.where(c == 0, picked[:part], picked[part:])
        give[place, :part, :] = jnp.where(c == 0, picked[part:], picked[:part])
    for k in range(PANELS):
        p = order[k]
        here = (p % N_PROW) == r
        block = rows[pl.ds(pl.multiple_of((p // N_PROW) * B, B), B), :]
        block = jnp.where(here, block, 0.0)
        place = lax.rem(k - y + NY, NY)
        keep[place, part:, :] = jnp.where(c == 0, block[:part], block[part:])
        give[place, part:, :] = jnp.where(c == 0, block[part:], block[:part])
    for t in range(BR):
        here = slice(t * B, (t + 1) * B)
        taken = is_target(target_row, B, (t * N_PROW + r) * B)
        rows[here, :] = jnp.where(taken, 0.0, rows[here, :])


def is_target(target_row, count, start):
    hot = jnp.where(iota((count, S), 0) + start == target_row[...], 1.0, 0.0)
    return jnp.max(hot, axis=1, keepdims=True) > 0.0


def add_kernel(keep, received, *sums):
    for u in range(NY):
        sums[u][...] = keep[u] + received[u]


def sum_kernel(pos, part0, part1, part2, part3, total, *chunks):
    x = pos[3]
    total[...] = (part0[...] + part1[...]) + (part2[...] + part3[...])
    count = CHUNK // 2
    for u in range(NX):
        start = lax.rem(x + u, NX) * count
        chunks[u][:count, :] = total[pl.ds(pl.multiple_of(start, count), count), :]
        chunks[u][count:, :] = total[pl.ds(pl.multiple_of(S // N_PROW + start, count), count), :]


def select_kernel(
    pos, order, width, pattern, target_row, spread, chunk0, chunk1, chunk2, chunk3, out
):
    r = pos[0]
    z = pos[2]
    x = pos[3]
    block_row = z * N_PROW + r
    taken = is_target(target_row, CHUNK, block_row * B + x * CHUNK)
    for k in range(PANELS):
        p = order[k]
        source = lax.rem(p, N_PCOL)
        cols = slice(k * B, (k + 1) * B)
        value = jnp.where(
            p >= N_PCOL,
            spread[source, pl.ds(1, CHUNK, stride=2), :],
            spread[source, pl.ds(0, CHUNK, stride=2), :],
        )
        value = kept(
            value, pattern[block_row, p] > 0, width[block_row], width[p], block_row == p, x * CHUNK
        )
        value = jnp.where(taken, 0.0, value)
        for j in range(NZ):
            out[j, :CHUNK, cols] = value
        value = jnp.zeros((CHUNK, B), F32)
        for u, chunk in enumerate((chunk0, chunk1, chunk2, chunk3)):
            here = source == z * NX + lax.rem(x - u + NX, NX)
            value = jnp.where(here & (p < N_PCOL), chunk[:, :B], value)
            value = jnp.where(here & (p >= N_PCOL), chunk[:, B:], value)
        for j in range(NZ):
            out[j, CHUNK:, cols] = value


def split_kernel(pieces, strips, rows):
    value = pieces[0, CHUNK:, :]
    for i in range(1, NZ):
        value = value + pieces[i, CHUNK:, :]
    rows[...] = value
    for i in range(NZ):
        strips[i] = pieces[i, :CHUNK, :]


def panel_order_rows(pos, same_core, other_core, first, out):
    c = pos[4]
    x = pos[3]
    y = lax.div(pos[0], NC)
    count = CHUNK // 2
    for u in range(NY):
        other_y = lax.rem(y - u + NY, NY)
        for core, group in ((c, same_core), (1 - c, other_core)):
            for j in range(NX):
                other_x = lax.rem(x - j + NX, NX)
                start = ((other_y * NC + core) * NX + other_x) * count
                out[pl.ds(pl.multiple_of(start, count), count), :] = group[u, j, first : first + count, :]


def prow_order(pos, same_core, other_core, first, out):
    c = pos[4]
    y = lax.div(pos[0], NC)
    part = S // N_PROW
    for u in range(NY):
        other_y = lax.rem(y - u + NY, NY)
        for core, group in ((c, same_core), (1 - c, other_core)):
            start = pl.multiple_of((other_y * NC + core) * part, part)
            out[pl.ds(start, part), :] = group[u, first : first + part, :]


def panels_here(pos, order):
    found = [jnp.int32(-1), jnp.int32(-1)]
    for s in range(2):
        for k in range(PANELS):
            found[s] = jnp.where(order[k] == s * N_PCOL + pos[1], k, found[s])
    return found


def quick_invert(corner):
    row = iota((B, B), 0)
    col = iota((B, B), 1)
    eye = jnp.where(row == col, 1.0, 0.0)
    diagonal = jnp.where(row == col, corner, 0.0)
    by_col = 1.0 / jnp.sum(diagonal, axis=0, keepdims=True)
    by_row = 1.0 / jnp.sum(diagonal, axis=1, keepdims=True)
    corner_parts = split2(corner)
    approx = by_row * (eye + (eye - corner * by_col))
    high, low = split2(approx)
    residual = eye - dot3(corner_parts, (high, low))
    approx = approx + dot_bf16(high, residual.astype(BF16))
    residual = eye - dot_full(corner, approx)
    error = jnp.sum(residual * residual)
    return approx + dot_bf16(approx.astype(BF16), residual.astype(BF16)), error


def invert(corner, work, pivot_rows, out):
    row = iota((B, B), 0)
    col = iota((B, B), 1)
    eye = jnp.where(row == col, 1.0, 0.0)
    diagonal = jnp.where(row == col, corner, 0.0)
    by_col = 1.0 / jnp.sum(diagonal, axis=0, keepdims=True)
    by_row = 1.0 / jnp.sum(diagonal, axis=1, keepdims=True)
    residual = eye - corner * by_col
    approx = by_row * (eye + residual)

    def sweep(state):
        count, error, approx = state
        residual = eye - dot_full(corner, approx)
        return count + 1, jnp.max(jnp.abs(residual)), approx + dot_full(approx, residual)

    def again(state):
        count, error, approx = state
        return (count < 16) & jnp.logical_not(error < 1e-5)

    count, error, approx = lax.while_loop(again, sweep, (0, jnp.float32(1.0), approx))
    out[...] = approx

    @pl.when(jnp.logical_not(error < 1e-5))
    def _():
        work[:, :B] = corner
        work[:, B:] = eye
        row1 = iota((B, 1), 0)
        lane = iota((1, 2 * B), 1)

        def step(i, used):
            column = jnp.sum(jnp.where(iota((B, 2 * B), 1) == i, work[...], 0.0), axis=1, keepdims=True)
            size = jnp.where(used > 0.0, -1.0, jnp.abs(column))
            biggest = jnp.max(size)
            at = jnp.min(jnp.where(size == biggest, row1, B - 1))
            pivot_rows[i] = at
            line = jnp.sum(jnp.where(row1 == at, work[...], 0.0), axis=0, keepdims=True)
            line = line / jnp.sum(jnp.where(lane == i, line, 0.0))
            work[...] = jnp.where(row1 == at, line, work[...] - column * line)
            return jnp.where(row1 == at, 1.0, used)

        lax.fori_loop(0, B, step, jnp.zeros((B, 1), F32))

        def place(i, carry):
            line = jnp.sum(jnp.where(row1 == pivot_rows[i], work[:, B:], 0.0), axis=0, keepdims=True)
            out[...] = jnp.where(row1 == i, line, out[...])
            return carry

        lax.fori_loop(0, B, place, 0)


def corner_kernel(
    pos, order, few, few_other, owns, owns_other,
    factor, upper, steps_high, steps_low, inverses, work, solver, steps, pivot_rows,
):
    def eliminate(invert_block):
        panel_order_rows(pos, few, few_other, 0, factor)
        prow_order(pos, owns, owns_other, 0, upper)
        solver[...] = jnp.zeros((S, S), F32)
        error = jnp.float32(0.0)
        for k in range(PANELS):
            here = slice(k * B, (k + 1) * B)
            later = slice((k + 1) * B, S)
            before = slice(0, k * B)
            inverse, found = invert_block(factor[here, here])
            error = error + found
            inverse_parts = split2(inverse)
            solver[here, here] = inverse
            if k + 1 < PANELS:
                lower = dot3(split2(factor[later, here]), inverse_parts)
                factor[later, here] = lower
                lower_parts = split2(lower)
                factor[later, later] = factor[later, later] - dot3(lower_parts, split2(factor[here, later]))
                upper[later, :] = upper[later, :] - dot3(lower_parts, split2(upper[here, :]))
            if k:
                above = dot3(split2(solver[before, before]), split2(factor[before, here]))
                solver[before, here] = -dot3(split2(above), inverse_parts)
        return error

    def robust(corner):
        invert(corner, work, pivot_rows, inverses)
        return inverses[...], jnp.float32(0.0)

    error = eliminate(quick_invert)

    @pl.when(jnp.logical_not(error < 1e-6))
    def _():
        eliminate(robust)

    steps[...] = dot3(split2(solver[...]), split2(upper[...]))
    found = panels_here(pos, order)
    for s in range(2):

        @pl.when(found[s] >= 0)
        def _():
            steps[:, s * B : (s + 1) * B] = -solver[:, pl.ds(pl.multiple_of(found[s] * B, B), B)]

    high, low = split2(steps[...])
    steps_high[...] = high
    steps_low[...] = low


def update_kernel(
    pos, order, target_row, rows, part0, part1, part2, part3, few, few_other, owns, owns_other,
    factor, upper, steps_high, steps_low,
    out, taken, home_rows, homes,
):
    r = pos[0]
    x = pos[3]
    half = S // 2
    steps_parts = (steps_high[...], steps_low[...])
    found = panels_here(pos, order)
    panel_order_rows(pos, few, few_other, CHUNK // 2, home_rows)
    prow_order(pos, owns, owns_other, S // N_PROW, homes)

    for i in range(2):
        here = slice(i * half, (i + 1) * half)
        product = dot3(split2(home_rows[here, :]), steps_parts)
        for s in range(2):
            cols = slice(s * B, (s + 1) * B)
            homes[here, cols] = jnp.where(found[s] >= 0, 0.0, homes[here, cols]) - product[:, cols]
    for u, part in enumerate((part0, part1, part2, part3)):
        product = dot3(split2(part[...].reshape(NZ * CHUNK, S)), steps_parts)
        other_x = lax.rem(x - u + NX, NX)
        for i in range(NZ):
            place = pl.ds(pl.multiple_of(i * B + other_x * CHUNK, CHUNK), CHUNK)
            taken[place, :] = product[i * CHUNK : (i + 1) * CHUNK]

    home_parts = split3(homes[...])
    for t in range(BR):
        block_row = t * N_PROW + r
        here = slice(t * B, (t + 1) * B)
        hot = (iota((B, S), 0) + block_row * B) == target_row[...]
        hot = jnp.where(hot, 1.0, 0.0).astype(BF16)
        moved = dot_bf16(hot, home_parts[0]) + (dot_bf16(hot, home_parts[1]) + dot_bf16(hot, home_parts[2]))
        for s in range(2):
            cols = slice(s * B, (s + 1) * B)
            value = jnp.where(found[s] >= 0, 0.0, rows[here, cols])
            out[pl.ds(t * 2 * B + s, B, stride=2), :] = (value - taken[here, cols]) + moved[:, cols]

    for k in range(PANELS):

        @pl.when(lax.rem(order[k], N_PROW) == r)
        def _():
            t = lax.div(order[k], N_PROW)
            here = slice(k * B, (k + 1) * B)
            for s in range(2):
                at = pl.multiple_of(jnp.maximum(found[s], 0) * B, B)
                value = jnp.where(
                    found[s] >= 0, factor[here, pl.ds(at, B)], upper[here, s * B : (s + 1) * B]
                )
                out[pl.ds(t * 2 * B + s, B, stride=2), :] = value


def call(kernel, smem, vmem, out_shapes, scratch):
    in_specs = [pl.BlockSpec(memory_space=pltpu.SMEM)] * len(smem)
    in_specs += [pl.BlockSpec(memory_space=pltpu.VMEM)] * len(vmem)
    return pl.pallas_call(
        kernel,
        out_shape=[jax.ShapeDtypeStruct(shape, kind) for kind, shape in out_shapes],
        in_specs=in_specs,
        out_specs=[pl.BlockSpec(memory_space=pltpu.VMEM)] * len(out_shapes),
        scratch_shapes=scratch,
        compiler_params=pltpu.CompilerParams(vmem_limit_bytes=VMEM_LIMIT),
    )(*smem, *vmem)


def shift(value, axis, size, by):
    return lax.ppermute(value, axis, [(i, (i + by) % size) for i in range(size)])


def gather(value, axis, size):
    return jnp.stack([value] + [shift(value, axis, size, i) for i in range(1, size)])


def body(matrix, node_width, block_pattern, pivot_row_targets, panel_order):
    z = lax.axis_index("z")
    x = lax.axis_index("x")
    c = lax.axis_index("c")
    r = lax.axis_index("y") * NC + c
    pos = jnp.stack([r, z * NX + x, z, x, c]).astype(jnp.int32)
    raw = matrix.reshape(ROWS * 2, B)
    target_col = pivot_row_targets.reshape(S, 1)
    target_row = pivot_row_targets.reshape(1, S)
    where = [pos, panel_order, node_width, block_pattern]
    part = S // N_PROW

    spread = lax.all_to_all(raw.reshape(N_PCOL, CHUNK * 2, B), ("z", "x"), 0, 0)
    keep, give, rows = call(
        own_rows_kernel,
        where,
        [target_col, target_row, raw],
        [(F32, (NY, 2 * part, 2 * B)), (F32, (NY, 2 * part, 2 * B)), (F32, (ROWS, 2 * B))],
        [],
    )
    sums = call(
        add_kernel, [], [keep, shift(give, "c", NC, 1)], [(F32, (2 * part, 2 * B))] * NY, []
    )
    sums = [sums[0]] + [shift(sums[u], "y", NY, u) for u in range(1, NY)]
    total, *chunks = call(
        sum_kernel,
        [pos],
        sums,
        [(F32, (2 * part, 2 * B))] + [(F32, (CHUNK, 2 * B))] * NX,
        [],
    )
    chunks = [chunks[0]] + [shift(chunks[u], "x", NX, u) for u in range(1, NX)]
    owns = gather(total, "y", NY)
    owns_other = shift(owns, "c", NC, 1)

    (pieces,) = call(
        select_kernel, where, [target_row, spread, *chunks], [(F32, (NZ, 2 * CHUNK, S))], []
    )
    pieces = lax.all_to_all(pieces, "z", 0, 0)
    pieces, owns_other = lax.optimization_barrier((pieces, owns_other))
    strips, few = call(split_kernel, [], [pieces], [(F32, (NZ, CHUNK, S)), (F32, (CHUNK, S))], [])
    parts = [strips] + [shift(strips, "x", NX, u) for u in range(1, NX)]
    few = gather(gather(few, "x", NX), "y", NY)
    few, parts[1], parts[3] = lax.optimization_barrier((few, parts[1], parts[3]))
    few_other = shift(few, "c", NC, 1)
    solved = call(
        corner_kernel,
        [pos, panel_order],
        [few, few_other, owns, owns_other],
        [(F32, (S, S)), (F32, (S, 2 * B)), (BF16, (S, 2 * B)), (BF16, (S, 2 * B))],
        [
            pltpu.VMEM((B, B), F32),
            pltpu.VMEM((B, 2 * B), F32),
            pltpu.VMEM((S, S), F32),
            pltpu.VMEM((S, 2 * B), F32),
            pltpu.SMEM((B,), jnp.int32),
        ],
    )
    (out,) = call(
        update_kernel,
        [pos, panel_order],
        [target_row, rows, *parts, few, few_other, owns, owns_other, *solved],
        [(F32, (ROWS * 2, B))],
        [pltpu.VMEM((ROWS, 2 * B), F32), pltpu.VMEM((S, S), F32), pltpu.VMEM((S, 2 * B), F32)],
    )
    return out.reshape(matrix.shape)


def solution(mesh):
    fine = Mesh(mesh.devices.reshape(NZ, NX, NY, NC), ("z", "x", "y", "c"))
    spec = P(None, ("y", "c"), None, None, ("z", "x"), None)
    return jax.shard_map(
        body,
        mesh=fine,
        in_specs=(spec, P(), P(), P(), P()),
        out_specs=spec,
        check_vma=False,
    )
```

```python
import jax
import jax.numpy as jnp
from jax import lax
from jax.experimental import pallas as pl
from jax.experimental.pallas import tpu as pltpu
from jax.sharding import Mesh, PartitionSpec as P

B = 128
PANELS = 4
S = PANELS * B
BR = 8
N_PROW = 8
N_PCOL = 32
NZ, NX, NY, NC = 8, 4, 4, 2
ROWS = BR * B
CHUNK = ROWS // N_PCOL
VMEM_LIMIT = 40 * 1024 * 1024
HIGHEST = lax.Precision.HIGHEST
F32 = jnp.float32
BF16 = jnp.bfloat16


def iota(shape, dim):
    return lax.broadcasted_iota(jnp.int32, shape, dim)


def dot_full(a, b):
    return jnp.dot(a, b, precision=HIGHEST, preferred_element_type=F32)


def dot_bf16(a, b):
    return jnp.dot(a, b, preferred_element_type=F32)


def split2(v):
    high = v.astype(BF16)
    low = (v - high.astype(F32)).astype(BF16)
    return high, low


def split3(v):
    high = v.astype(BF16)
    rest = v - high.astype(F32)
    middle = rest.astype(BF16)
    low = (rest - middle.astype(F32)).astype(BF16)
    return high, middle, low


def dot3(a, b):
    return dot_bf16(a[0], b[0]) + (dot_bf16(a[0], b[1]) + dot_bf16(a[1], b[0]))


def kept(value, here, row_width, col_width, same_block, row_start):
    rows = iota(value.shape, 0) + row_start
    cols = iota(value.shape, 1)
    value = jnp.where(here & (rows < row_width) & (cols < col_width), value, 0.0)
    return jnp.where(same_block & (rows == cols) & (rows >= row_width), 1.0, value)


def own_rows_kernel(pos, order, width, pattern, target_col, target_row, raw, keep, give, rows):
    r = pos[0]
    q = pos[1]
    c = pos[4]
    y = lax.div(r, NC)
    for t in range(BR):
        block_row = t * N_PROW + r
        for s in range(2):
            block_col = s * N_PCOL + q
            rows[t * B : (t + 1) * B, s * B : (s + 1) * B] = kept(
                raw[pl.ds(t * 2 * B + s, B, stride=2), :],
                pattern[block_row, block_col] > 0,
                width[block_row],
                width[block_col],
                block_row == block_col,
                0,
            )
    part = S // N_PROW
    high, middle, low = split3(rows[...])
    lane = iota((B, ROWS), 1)
    row_id = ((lane // B) * N_PROW + r) * B + lane % B
    for i in range(0, S, B):
        hot = jnp.where(row_id == target_col[i : i + B, :], 1.0, 0.0).astype(BF16)
        picked = dot_bf16(hot, high) + (dot_bf16(hot, middle) + dot_bf16(hot, low))
        place = lax.rem(i // B - y + NY, NY)
        keep[place, :part, :] = jnp.where(c == 0, picked[:part], picked[part:])
        give[place, :part, :] = jnp.where(c == 0, picked[part:], picked[:part])
    for k in range(PANELS):
        p = order[k]
        here = (p % N_PROW) == r
        block = rows[pl.ds(pl.multiple_of((p // N_PROW) * B, B), B), :]
        block = jnp.where(here, block, 0.0)
        place = lax.rem(k - y + NY, NY)
        keep[place, part:, :] = jnp.where(c == 0, block[:part], block[part:])
        give[place, part:, :] = jnp.where(c == 0, block[part:], block[:part])
    for t in range(BR):
        here = slice(t * B, (t + 1) * B)
        taken = is_target(target_row, B, (t * N_PROW + r) * B)
        rows[here, :] = jnp.where(taken, 0.0, rows[here, :])


def is_target(target_row, count, start):
    hot = jnp.where(iota((count, S), 0) + start == target_row[...], 1.0, 0.0)
    return jnp.max(hot, axis=1, keepdims=True) > 0.0


def add_kernel(keep, received, *sums):
    for u in range(NY):
        sums[u][...] = keep[u] + received[u]


def sum_kernel(pos, part0, part1, part2, part3, total, *chunks):
    x = pos[3]
    total[...] = (part0[...] + part1[...]) + (part2[...] + part3[...])
    count = CHUNK // 2
    for u in range(NX):
        start = lax.rem(x + u, NX) * count
        chunks[u][:count, :] = total[pl.ds(pl.multiple_of(start, count), count), :]
        chunks[u][count:, :] = total[pl.ds(pl.multiple_of(S // N_PROW + start, count), count), :]


def select_kernel(pos, order, width, pattern, target_row, spread, out):
    r = pos[0]
    z = pos[2]
    x = pos[3]
    block_row = z * N_PROW + r
    taken = is_target(target_row, CHUNK, block_row * B + x * CHUNK)
    for k in range(PANELS):
        p = order[k]
        source = lax.rem(p, N_PCOL)
        value = jnp.where(
            p >= N_PCOL,
            spread[source, pl.ds(1, CHUNK, stride=2), :],
            spread[source, pl.ds(0, CHUNK, stride=2), :],
        )
        value = kept(
            value, pattern[block_row, p] > 0, width[block_row], width[p], block_row == p, x * CHUNK
        )
        value = jnp.where(taken, 0.0, value)
        for j in range(NZ):
            out[j, :, k * B : (k + 1) * B] = value


def select_few_kernel(pos, order, chunk0, chunk1, chunk2, chunk3, out):
    z = pos[2]
    x = pos[3]
    for k in range(PANELS):
        p = order[k]
        source = lax.rem(p, N_PCOL)
        value = jnp.zeros((CHUNK, B), F32)
        for u, chunk in enumerate((chunk0, chunk1, chunk2, chunk3)):
            here = source == z * NX + lax.rem(x - u + NX, NX)
            value = jnp.where(here & (p < N_PCOL), chunk[:, :B], value)
            value = jnp.where(here & (p >= N_PCOL), chunk[:, B:], value)
        out[:, k * B : (k + 1) * B] = value


def add_two_kernel(a, b, out):
    out[...] = a[...] + b[...]


def add_four_kernel(a, b, c, d, out):
    out[...] = (a[...] + b[...]) + (c[...] + d[...])


def panel_order_rows(pos, same_core, other_core, first, out):
    c = pos[4]
    x = pos[3]
    y = lax.div(pos[0], NC)
    count = CHUNK // 2
    for u in range(NY):
        other_y = lax.rem(y - u + NY, NY)
        for core, group in ((c, same_core), (1 - c, other_core)):
            for j in range(NX):
                other_x = lax.rem(x - j + NX, NX)
                start = pl.multiple_of(((other_y * NC + core) * NX + other_x) * count, count)
                rows = slice(j * CHUNK + first, j * CHUNK + first + count)
                out[pl.ds(start, count), :] = group[u, rows, :S]


def own_order_rows(pos, same_core, other_core, first, out):
    c = pos[4]
    y = lax.div(pos[0], NC)
    part = S // N_PROW
    for u in range(NY):
        other_y = lax.rem(y - u + NY, NY)
        for core, group in ((c, same_core), (1 - c, other_core)):
            start = pl.multiple_of((other_y * NC + core) * part, part)
            out[pl.ds(start, part), :] = group[u, first : first + part, S:]


def panels_here(pos, order):
    found = [jnp.int32(-1), jnp.int32(-1)]
    for s in range(2):
        for k in range(PANELS):
            found[s] = jnp.where(order[k] == s * N_PCOL + pos[1], k, found[s])
    return found


def quick_invert(corner):
    row = iota((B, B), 0)
    col = iota((B, B), 1)
    eye = jnp.where(row == col, 1.0, 0.0)
    diagonal = jnp.where(row == col, corner, 0.0)
    by_col = 1.0 / jnp.sum(diagonal, axis=0, keepdims=True)
    by_row = 1.0 / jnp.sum(diagonal, axis=1, keepdims=True)
    corner_parts = split2(corner)
    approx = by_row * (eye + (eye - corner * by_col))
    high, low = split2(approx)
    residual = eye - dot3(corner_parts, (high, low))
    approx = approx + dot_bf16(high, residual.astype(BF16))
    residual = eye - dot_full(corner, approx)
    error = jnp.sum(residual * residual)
    return approx + dot_bf16(approx.astype(BF16), residual.astype(BF16)), error


def invert(corner, work, pivot_rows, out):
    row = iota((B, B), 0)
    col = iota((B, B), 1)
    eye = jnp.where(row == col, 1.0, 0.0)
    diagonal = jnp.where(row == col, corner, 0.0)
    by_col = 1.0 / jnp.sum(diagonal, axis=0, keepdims=True)
    by_row = 1.0 / jnp.sum(diagonal, axis=1, keepdims=True)
    residual = eye - corner * by_col
    approx = by_row * (eye + residual)

    def sweep(state):
        count, error, approx = state
        residual = eye - dot_full(corner, approx)
        return count + 1, jnp.max(jnp.abs(residual)), approx + dot_full(approx, residual)

    def again(state):
        count, error, approx = state
        return (count < 16) & jnp.logical_not(error < 1e-5)

    count, error, approx = lax.while_loop(again, sweep, (0, jnp.float32(1.0), approx))
    out[...] = approx

    @pl.when(jnp.logical_not(error < 1e-5))
    def _():
        work[:, :B] = corner
        work[:, B:] = eye
        row1 = iota((B, 1), 0)
        lane = iota((1, 2 * B), 1)

        def step(i, used):
            column = jnp.sum(jnp.where(iota((B, 2 * B), 1) == i, work[...], 0.0), axis=1, keepdims=True)
            size = jnp.where(used > 0.0, -1.0, jnp.abs(column))
            biggest = jnp.max(size)
            at = jnp.min(jnp.where(size == biggest, row1, B - 1))
            pivot_rows[i] = at
            line = jnp.sum(jnp.where(row1 == at, work[...], 0.0), axis=0, keepdims=True)
            line = line / jnp.sum(jnp.where(lane == i, line, 0.0))
            work[...] = jnp.where(row1 == at, line, work[...] - column * line)
            return jnp.where(row1 == at, 1.0, used)

        lax.fori_loop(0, B, step, jnp.zeros((B, 1), F32))

        def place(i, carry):
            line = jnp.sum(jnp.where(row1 == pivot_rows[i], work[:, B:], 0.0), axis=0, keepdims=True)
            out[...] = jnp.where(row1 == i, line, out[...])
            return carry

        lax.fori_loop(0, B, place, 0)


def corner_kernel(
    pos, order, few, few_other,
    factor, upper, steps_high, steps_low, inverses, work, solver, steps, pivot_rows,
):
    def eliminate(invert_block):
        panel_order_rows(pos, few, few_other, 0, factor)
        own_order_rows(pos, few, few_other, 0, upper)
        solver[...] = jnp.zeros((S, S), F32)
        error = jnp.float32(0.0)
        for k in range(PANELS):
            here = slice(k * B, (k + 1) * B)
            later = slice((k + 1) * B, S)
            before = slice(0, k * B)
            inverse, found = invert_block(factor[here, here])
            error = error + found
            inverse_parts = split2(inverse)
            solver[here, here] = inverse
            if k + 1 < PANELS:
                lower = dot3(split2(factor[later, here]), inverse_parts)
                factor[later, here] = lower
                lower_parts = split2(lower)
                factor[later, later] = factor[later, later] - dot3(lower_parts, split2(factor[here, later]))
                upper[later, :] = upper[later, :] - dot3(lower_parts, split2(upper[here, :]))
            if k:
                above = dot3(split2(solver[before, before]), split2(factor[before, here]))
                solver[before, here] = -dot3(split2(above), inverse_parts)
        return error

    def robust(corner):
        invert(corner, work, pivot_rows, inverses)
        return inverses[...], jnp.float32(0.0)

    error = eliminate(quick_invert)

    @pl.when(jnp.logical_not(error < 1e-6))
    def _():
        eliminate(robust)

    steps[...] = dot3(split2(solver[...]), split2(upper[...]))
    found = panels_here(pos, order)
    for s in range(2):

        @pl.when(found[s] >= 0)
        def _():
            steps[:, s * B : (s + 1) * B] = -solver[:, pl.ds(pl.multiple_of(found[s] * B, B), B)]

    high, low = split2(steps[...])
    steps_high[...] = high
    steps_low[...] = low


def update_kernel(
    pos, order, target_row, rows, part0, part1, part2a, part2b, part3, few, few_other,
    factor, upper, steps_high, steps_low,
    out, taken, home_rows, homes,
):
    r = pos[0]
    x = pos[3]
    half = S // 2
    steps_parts = (steps_high[...], steps_low[...])
    found = panels_here(pos, order)
    panel_order_rows(pos, few, few_other, CHUNK // 2, home_rows)
    own_order_rows(pos, few, few_other, S // N_PROW, homes)

    for i in range(2):
        here = slice(i * half, (i + 1) * half)
        product = dot3(split2(home_rows[here, :]), steps_parts)
        for s in range(2):
            cols = slice(s * B, (s + 1) * B)
            homes[here, cols] = jnp.where(found[s] >= 0, 0.0, homes[here, cols]) - product[:, cols]
    part2 = jnp.concatenate([part2a[...], part2b[...]], axis=0)
    for u, part in enumerate((part0[...], part1[...], part2, part3[...])):
        product = dot3(split2(part.reshape(NZ * CHUNK, S)), steps_parts)
        other_x = lax.rem(x - u + NX, NX)
        for i in range(NZ):
            place = pl.ds(pl.multiple_of(i * B + other_x * CHUNK, CHUNK), CHUNK)
            taken[place, :] = product[i * CHUNK : (i + 1) * CHUNK]

    home_parts = split3(homes[...])
    for t in range(BR):
        block_row = t * N_PROW + r
        here = slice(t * B, (t + 1) * B)
        hot = (iota((B, S), 0) + block_row * B) == target_row[...]
        hot = jnp.where(hot, 1.0, 0.0).astype(BF16)
        moved = dot_bf16(hot, home_parts[0]) + (dot_bf16(hot, home_parts[1]) + dot_bf16(hot, home_parts[2]))
        for s in range(2):
            cols = slice(s * B, (s + 1) * B)
            value = jnp.where(found[s] >= 0, 0.0, rows[here, cols])
            out[pl.ds(t * 2 * B + s, B, stride=2), :] = (value - taken[here, cols]) + moved[:, cols]

    for k in range(PANELS):

        @pl.when(lax.rem(order[k], N_PROW) == r)
        def _():
            t = lax.div(order[k], N_PROW)
            here = slice(k * B, (k + 1) * B)
            for s in range(2):
                at = pl.multiple_of(jnp.maximum(found[s], 0) * B, B)
                value = jnp.where(
                    found[s] >= 0, factor[here, pl.ds(at, B)], upper[here, s * B : (s + 1) * B]
                )
                out[pl.ds(t * 2 * B + s, B, stride=2), :] = value


def call(kernel, smem, vmem, out_shapes, scratch):
    in_specs = [pl.BlockSpec(memory_space=pltpu.SMEM)] * len(smem)
    in_specs += [pl.BlockSpec(memory_space=pltpu.VMEM)] * len(vmem)
    return pl.pallas_call(
        kernel,
        out_shape=[jax.ShapeDtypeStruct(shape, kind) for kind, shape in out_shapes],
        in_specs=in_specs,
        out_specs=[pl.BlockSpec(memory_space=pltpu.VMEM)] * len(out_shapes),
        scratch_shapes=scratch,
        compiler_params=pltpu.CompilerParams(vmem_limit_bytes=VMEM_LIMIT),
    )(*smem, *vmem)


def shift(value, axis, size, by):
    return lax.ppermute(value, axis, [(i, (i + by) % size) for i in range(size)])


def gather(value, axis, size):
    return jnp.stack([value] + [shift(value, axis, size, i) for i in range(1, size)])


def body(matrix, node_width, block_pattern, pivot_row_targets, panel_order):
    z = lax.axis_index("z")
    x = lax.axis_index("x")
    c = lax.axis_index("c")
    r = lax.axis_index("y") * NC + c
    pos = jnp.stack([r, z * NX + x, z, x, c]).astype(jnp.int32)
    raw = matrix.reshape(ROWS * 2, B)
    target_col = pivot_row_targets.reshape(S, 1)
    target_row = pivot_row_targets.reshape(1, S)
    where = [pos, panel_order, node_width, block_pattern]
    part = S // N_PROW

    spread = lax.all_to_all(raw.reshape(N_PCOL, CHUNK * 2, B), ("z", "x"), 0, 0)
    keep, give, rows = call(
        own_rows_kernel,
        where,
        [target_col, target_row, raw],
        [(F32, (NY, 2 * part, 2 * B)), (F32, (NY, 2 * part, 2 * B)), (F32, (ROWS, 2 * B))],
        [],
    )
    sums = call(
        add_kernel, [], [keep, shift(give, "c", NC, 1)], [(F32, (2 * part, 2 * B))] * NY, []
    )
    sums = [sums[0]] + [shift(sums[u], "y", NY, u) for u in range(1, NY)]
    total, *chunks = call(
        sum_kernel,
        [pos],
        sums,
        [(F32, (2 * part, 2 * B))] + [(F32, (CHUNK, 2 * B))] * NX,
        [],
    )
    chunks = [chunks[0]] + [shift(chunks[u], "x", NX, u) for u in range(1, NX)]

    (few,) = call(select_few_kernel, [pos, panel_order], chunks, [(F32, (CHUNK, S))], [])
    near = lax.ppermute(few, "z", [(i, i ^ 1) for i in range(NZ)])
    (few,) = call(add_two_kernel, [], [few, near], [(F32, (CHUNK, S))], [])
    (strip,) = call(select_kernel, where, [target_row, spread], [(F32, (NZ, CHUNK, S))], [])
    few, strip = lax.optimization_barrier((few, strip))
    far = [shift(few, "z", NZ, i) for i in (2, 4, 6)]
    (few,) = call(add_four_kernel, [], [few, *far], [(F32, (CHUNK, S))], [])
    few, strip = lax.optimization_barrier((few, strip))
    strips = lax.all_to_all(strip, "z", 0, 0)
    few = gather(few, "x", NX)
    part1 = shift(strips, "x", NX, 1)
    part3 = shift(strips, "x", NX, 3)
    few = jnp.concatenate([few.reshape(NX * CHUNK, S), total], axis=1)
    few = gather(few, "y", NY)
    few, part1, part3 = lax.optimization_barrier((few, part1, part3))
    few_other = shift(few, "c", NC, 1)
    half = NZ // 2
    parts = [strips, part1, shift(part1[:half], "x", NX, 1), shift(part3[half:], "x", NX, 3), part3]
    solved = call(
        corner_kernel,
        [pos, panel_order],
        [few, few_other],
        [(F32, (S, S)), (F32, (S, 2 * B)), (BF16, (S, 2 * B)), (BF16, (S, 2 * B))],
        [
            pltpu.VMEM((B, B), F32),
            pltpu.VMEM((B, 2 * B), F32),
            pltpu.VMEM((S, S), F32),
            pltpu.VMEM((S, 2 * B), F32),
            pltpu.SMEM((B,), jnp.int32),
        ],
    )
    (out,) = call(
        update_kernel,
        [pos, panel_order],
        [target_row, rows, *parts, few, few_other, *solved],
        [(F32, (ROWS * 2, B))],
        [pltpu.VMEM((ROWS, 2 * B), F32), pltpu.VMEM((S, S), F32), pltpu.VMEM((S, 2 * B), F32)],
    )
    return out.reshape(matrix.shape)


def solution(mesh):
    fine = Mesh(mesh.devices.reshape(NZ, NX, NY, NC), ("z", "x", "y", "c"))
    spec = P(None, ("y", "c"), None, None, ("z", "x"), None)
    return jax.shard_map(
        body,
        mesh=fine,
        in_specs=(spec, P(), P(), P(), P()),
        out_specs=spec,
        check_vma=False,
    )
```

```python
import jax
import jax.numpy as jnp
from jax import lax
from jax.experimental import pallas as pl
from jax.experimental.pallas import tpu as pltpu
from jax.sharding import Mesh, PartitionSpec as P

B = 128
PANELS = 4
S = PANELS * B
BR = 8
N_PROW = 8
N_PCOL = 32
NZ, NX, NY, NC = 8, 4, 4, 2
ROWS = BR * B
CHUNK = ROWS // N_PCOL
VMEM_LIMIT = 40 * 1024 * 1024
HIGHEST = lax.Precision.HIGHEST
F32 = jnp.float32
BF16 = jnp.bfloat16


def iota(shape, dim):
    return lax.broadcasted_iota(jnp.int32, shape, dim)


def dot_full(a, b):
    return jnp.dot(a, b, precision=HIGHEST, preferred_element_type=F32)


def dot_bf16(a, b):
    return jnp.dot(a, b, preferred_element_type=F32)


def split2(v):
    high = v.astype(BF16)
    low = (v - high.astype(F32)).astype(BF16)
    return high, low


def split3(v):
    high = v.astype(BF16)
    rest = v - high.astype(F32)
    middle = rest.astype(BF16)
    low = (rest - middle.astype(F32)).astype(BF16)
    return high, middle, low


def dot3(a, b):
    return dot_bf16(a[0], b[0]) + (dot_bf16(a[0], b[1]) + dot_bf16(a[1], b[0]))


def kept(value, here, row_width, col_width, same_block, row_start):
    rows = iota(value.shape, 0) + row_start
    cols = iota(value.shape, 1)
    value = jnp.where(here & (rows < row_width) & (cols < col_width), value, 0.0)
    return jnp.where(same_block & (rows == cols) & (rows >= row_width), 1.0, value)


def own_rows_kernel(pos, order, width, pattern, target_col, raw, keep, give, rows):
    r = pos[0]
    q = pos[1]
    c = pos[4]
    y = lax.div(r, NC)
    for t in range(BR):
        block_row = t * N_PROW + r
        for s in range(2):
            block_col = s * N_PCOL + q
            rows[t * B : (t + 1) * B, s * B : (s + 1) * B] = kept(
                raw[pl.ds(t * 2 * B + s, B, stride=2), :],
                pattern[block_row, block_col] > 0,
                width[block_row],
                width[block_col],
                block_row == block_col,
                0,
            )
    part = S // N_PROW
    high, middle, low = split3(rows[...])
    lane = iota((B, ROWS), 1)
    row_id = ((lane // B) * N_PROW + r) * B + lane % B
    for i in range(0, S, B):
        hot = jnp.where(row_id == target_col[i : i + B, :], 1.0, 0.0).astype(BF16)
        picked = dot_bf16(hot, high) + (dot_bf16(hot, middle) + dot_bf16(hot, low))
        place = lax.rem(i // B - y + NY, NY)
        keep[place, :part, :] = jnp.where(c == 0, picked[:part], picked[part:])
        give[place, :part, :] = jnp.where(c == 0, picked[part:], picked[:part])
    for k in range(PANELS):
        p = order[k]
        here = (p % N_PROW) == r
        block = rows[pl.ds(pl.multiple_of((p // N_PROW) * B, B), B), :]
        block = jnp.where(here, block, 0.0)
        place = lax.rem(k - y + NY, NY)
        keep[place, part:, :] = jnp.where(c == 0, block[:part], block[part:])
        give[place, part:, :] = jnp.where(c == 0, block[part:], block[:part])


def is_target(target_row, count, start):
    hot = jnp.where(iota((count, S), 0) + start == target_row[...], 1.0, 0.0)
    return jnp.max(hot, axis=1, keepdims=True) > 0.0


def add_kernel(keep, received, *sums):
    for u in range(NY):
        sums[u][...] = keep[u] + received[u]


def sum_kernel(pos, part0, part1, part2, part3, total, *chunks):
    x = pos[3]
    total[...] = (part0[...] + part1[...]) + (part2[...] + part3[...])
    count = CHUNK // 2
    for u in range(NX):
        start = lax.rem(x + u, NX) * count
        chunks[u][:count, :] = total[pl.ds(pl.multiple_of(start, count), count), :]
        chunks[u][count:, :] = total[pl.ds(pl.multiple_of(S // N_PROW + start, count), count), :]


def select_kernel(pos, order, width, pattern, target_row, spread, own, out, rows, hots):
    r = pos[0]
    z = pos[2]
    x = pos[3]
    block_row = z * N_PROW + r
    taken = is_target(target_row, CHUNK, block_row * B + x * CHUNK)
    for k in range(PANELS):
        p = order[k]
        source = lax.rem(p, N_PCOL)
        value = jnp.where(
            p >= N_PCOL,
            spread[source, pl.ds(1, CHUNK, stride=2), :],
            spread[source, pl.ds(0, CHUNK, stride=2), :],
        )
        value = kept(
            value, pattern[block_row, p] > 0, width[block_row], width[p], block_row == p, x * CHUNK
        )
        value = jnp.where(taken, 0.0, value)
        for j in range(NZ):
            out[j, :, k * B : (k + 1) * B] = value
    for t in range(BR):
        here = slice(t * B, (t + 1) * B)
        hot = jnp.where(iota((B, S), 0) + (t * N_PROW + r) * B == target_row[...], 1.0, 0.0)
        taken = jnp.max(hot, axis=1, keepdims=True) > 0.0
        rows[here, :] = jnp.where(taken, 0.0, own[here, :])
        hots[here, :] = hot.astype(BF16)


def select_few_kernel(pos, order, chunk0, chunk1, chunk2, chunk3, out):
    z = pos[2]
    x = pos[3]
    for k in range(PANELS):
        p = order[k]
        source = lax.rem(p, N_PCOL)
        value = jnp.zeros((CHUNK, B), F32)
        for u, chunk in enumerate((chunk0, chunk1, chunk2, chunk3)):
            here = source == z * NX + lax.rem(x - u + NX, NX)
            value = jnp.where(here & (p < N_PCOL), chunk[:, :B], value)
            value = jnp.where(here & (p >= N_PCOL), chunk[:, B:], value)
        out[:, k * B : (k + 1) * B] = value


def add_two_kernel(a, b, out):
    out[...] = a[...] + b[...]


def add_four_kernel(a, b, c, d, out):
    out[...] = (a[...] + b[...]) + (c[...] + d[...])


def panel_order_rows(pos, same_core, other_core, first, out):
    c = pos[4]
    x = pos[3]
    y = lax.div(pos[0], NC)
    count = CHUNK // 2
    for u in range(NY):
        other_y = lax.rem(y - u + NY, NY)
        for core, group in ((c, same_core), (1 - c, other_core)):
            for j in range(NX):
                other_x = lax.rem(x - j + NX, NX)
                start = pl.multiple_of(((other_y * NC + core) * NX + other_x) * count, count)
                rows = slice(j * CHUNK + first, j * CHUNK + first + count)
                out[pl.ds(start, count), :] = group[u, rows, :S]


def own_order_rows(pos, same_core, other_core, first, out):
    c = pos[4]
    y = lax.div(pos[0], NC)
    part = S // N_PROW
    for u in range(NY):
        other_y = lax.rem(y - u + NY, NY)
        for core, group in ((c, same_core), (1 - c, other_core)):
            start = pl.multiple_of((other_y * NC + core) * part, part)
            out[pl.ds(start, part), :] = group[u, first : first + part, S:]


def panels_here(pos, order):
    found = [jnp.int32(-1), jnp.int32(-1)]
    for s in range(2):
        for k in range(PANELS):
            found[s] = jnp.where(order[k] == s * N_PCOL + pos[1], k, found[s])
    return found


def quick_invert(corner):
    row = iota((B, B), 0)
    col = iota((B, B), 1)
    eye = jnp.where(row == col, 1.0, 0.0)
    diagonal = jnp.where(row == col, corner, 0.0)
    by_col = 1.0 / jnp.sum(diagonal, axis=0, keepdims=True)
    by_row = 1.0 / jnp.sum(diagonal, axis=1, keepdims=True)
    corner_parts = split2(corner)
    approx = by_row * (eye + (eye - corner * by_col))
    high, low = split2(approx)
    residual = eye - dot3(corner_parts, (high, low))
    approx = approx + dot_bf16(high, residual.astype(BF16))
    residual = eye - dot_full(corner, approx)
    error = jnp.sum(residual * residual)
    return approx + dot_bf16(approx.astype(BF16), residual.astype(BF16)), error


def invert(corner, work, pivot_rows, out):
    row = iota((B, B), 0)
    col = iota((B, B), 1)
    eye = jnp.where(row == col, 1.0, 0.0)
    diagonal = jnp.where(row == col, corner, 0.0)
    by_col = 1.0 / jnp.sum(diagonal, axis=0, keepdims=True)
    by_row = 1.0 / jnp.sum(diagonal, axis=1, keepdims=True)
    residual = eye - corner * by_col
    approx = by_row * (eye + residual)

    def sweep(state):
        count, error, approx = state
        residual = eye - dot_full(corner, approx)
        return count + 1, jnp.max(jnp.abs(residual)), approx + dot_full(approx, residual)

    def again(state):
        count, error, approx = state
        return (count < 16) & jnp.logical_not(error < 1e-5)

    count, error, approx = lax.while_loop(again, sweep, (0, jnp.float32(1.0), approx))
    out[...] = approx

    @pl.when(jnp.logical_not(error < 1e-5))
    def _():
        work[:, :B] = corner
        work[:, B:] = eye
        row1 = iota((B, 1), 0)
        lane = iota((1, 2 * B), 1)

        def step(i, used):
            column = jnp.sum(jnp.where(iota((B, 2 * B), 1) == i, work[...], 0.0), axis=1, keepdims=True)
            size = jnp.where(used > 0.0, -1.0, jnp.abs(column))
            biggest = jnp.max(size)
            at = jnp.min(jnp.where(size == biggest, row1, B - 1))
            pivot_rows[i] = at
            line = jnp.sum(jnp.where(row1 == at, work[...], 0.0), axis=0, keepdims=True)
            line = line / jnp.sum(jnp.where(lane == i, line, 0.0))
            work[...] = jnp.where(row1 == at, line, work[...] - column * line)
            return jnp.where(row1 == at, 1.0, used)

        lax.fori_loop(0, B, step, jnp.zeros((B, 1), F32))

        def place(i, carry):
            line = jnp.sum(jnp.where(row1 == pivot_rows[i], work[:, B:], 0.0), axis=0, keepdims=True)
            out[...] = jnp.where(row1 == i, line, out[...])
            return carry

        lax.fori_loop(0, B, place, 0)


def corner_kernel(
    pos, order, few, few_other,
    factor, upper, steps_high, steps_low, inverses, work, solver, steps, pivot_rows,
):
    def eliminate(invert_block):
        panel_order_rows(pos, few, few_other, 0, factor)
        own_order_rows(pos, few, few_other, 0, upper)
        solver[...] = jnp.zeros((S, S), F32)
        error = jnp.float32(0.0)
        for k in range(PANELS):
            here = slice(k * B, (k + 1) * B)
            later = slice((k + 1) * B, S)
            before = slice(0, k * B)
            inverse, found = invert_block(factor[here, here])
            error = error + found
            inverse_parts = split2(inverse)
            solver[here, here] = inverse
            if k + 1 < PANELS:
                lower = dot3(split2(factor[later, here]), inverse_parts)
                factor[later, here] = lower
                lower_parts = split2(lower)
                factor[later, later] = factor[later, later] - dot3(lower_parts, split2(factor[here, later]))
                upper[later, :] = upper[later, :] - dot3(lower_parts, split2(upper[here, :]))
            if k:
                above = dot3(split2(solver[before, before]), split2(factor[before, here]))
                solver[before, here] = -dot3(split2(above), inverse_parts)
        return error

    def robust(corner):
        invert(corner, work, pivot_rows, inverses)
        return inverses[...], jnp.float32(0.0)

    error = eliminate(quick_invert)

    @pl.when(jnp.logical_not(error < 1e-6))
    def _():
        eliminate(robust)

    steps[...] = dot3(split2(solver[...]), split2(upper[...]))
    found = panels_here(pos, order)
    for s in range(2):

        @pl.when(found[s] >= 0)
        def _():
            steps[:, s * B : (s + 1) * B] = -solver[:, pl.ds(pl.multiple_of(found[s] * B, B), B)]

    high, low = split2(steps[...])
    steps_high[...] = high
    steps_low[...] = low


def update_kernel(
    pos, order, hots, rows, part0, part1, part2a, part2b, part3, few, few_other,
    factor, upper, steps_high, steps_low,
    out, taken, home_rows, homes,
):
    r = pos[0]
    x = pos[3]
    half = S // 2
    steps_parts = (steps_high[...], steps_low[...])
    found = panels_here(pos, order)
    panel_order_rows(pos, few, few_other, CHUNK // 2, home_rows)
    own_order_rows(pos, few, few_other, S // N_PROW, homes)

    for i in range(2):
        here = slice(i * half, (i + 1) * half)
        product = dot3(split2(home_rows[here, :]), steps_parts)
        for s in range(2):
            cols = slice(s * B, (s + 1) * B)
            homes[here, cols] = jnp.where(found[s] >= 0, 0.0, homes[here, cols]) - product[:, cols]
    part2 = jnp.concatenate([part2a[...], part2b[...]], axis=0)
    for u, part in enumerate((part0[...], part1[...], part2, part3[...])):
        product = dot3(split2(part.reshape(NZ * CHUNK, S)), steps_parts)
        other_x = lax.rem(x - u + NX, NX)
        for i in range(NZ):
            place = pl.ds(pl.multiple_of(i * B + other_x * CHUNK, CHUNK), CHUNK)
            taken[place, :] = product[i * CHUNK : (i + 1) * CHUNK]

    home_parts = split3(homes[...])
    for t in range(BR):
        here = slice(t * B, (t + 1) * B)
        hot = hots[here, :]
        moved = dot_bf16(hot, home_parts[0]) + (dot_bf16(hot, home_parts[1]) + dot_bf16(hot, home_parts[2]))
        for s in range(2):
            cols = slice(s * B, (s + 1) * B)
            value = jnp.where(found[s] >= 0, 0.0, rows[here, cols])
            out[pl.ds(t * 2 * B + s, B, stride=2), :] = (value - taken[here, cols]) + moved[:, cols]

    for k in range(PANELS):

        @pl.when(lax.rem(order[k], N_PROW) == r)
        def _():
            t = lax.div(order[k], N_PROW)
            here = slice(k * B, (k + 1) * B)
            for s in range(2):
                at = pl.multiple_of(jnp.maximum(found[s], 0) * B, B)
                value = jnp.where(
                    found[s] >= 0, factor[here, pl.ds(at, B)], upper[here, s * B : (s + 1) * B]
                )
                out[pl.ds(t * 2 * B + s, B, stride=2), :] = value


def call(kernel, smem, vmem, out_shapes, scratch):
    in_specs = [pl.BlockSpec(memory_space=pltpu.SMEM)] * len(smem)
    in_specs += [pl.BlockSpec(memory_space=pltpu.VMEM)] * len(vmem)
    return pl.pallas_call(
        kernel,
        out_shape=[jax.ShapeDtypeStruct(shape, kind) for kind, shape in out_shapes],
        in_specs=in_specs,
        out_specs=[pl.BlockSpec(memory_space=pltpu.VMEM)] * len(out_shapes),
        scratch_shapes=scratch,
        compiler_params=pltpu.CompilerParams(vmem_limit_bytes=VMEM_LIMIT),
    )(*smem, *vmem)


def shift(value, axis, size, by):
    return lax.ppermute(value, axis, [(i, (i + by) % size) for i in range(size)])


def gather(value, axis, size):
    return jnp.stack([value] + [shift(value, axis, size, i) for i in range(1, size)])


def body(matrix, node_width, block_pattern, pivot_row_targets, panel_order):
    z = lax.axis_index("z")
    x = lax.axis_index("x")
    c = lax.axis_index("c")
    r = lax.axis_index("y") * NC + c
    pos = jnp.stack([r, z * NX + x, z, x, c]).astype(jnp.int32)
    raw = matrix.reshape(ROWS * 2, B)
    target_col = pivot_row_targets.reshape(S, 1)
    target_row = pivot_row_targets.reshape(1, S)
    where = [pos, panel_order, node_width, block_pattern]
    part = S // N_PROW

    spread = lax.all_to_all(raw.reshape(N_PCOL, CHUNK * 2, B), ("z", "x"), 0, 0)
    keep, give, rows = call(
        own_rows_kernel,
        where,
        [target_col, raw],
        [(F32, (NY, 2 * part, 2 * B)), (F32, (NY, 2 * part, 2 * B)), (F32, (ROWS, 2 * B))],
        [],
    )
    sums = call(
        add_kernel, [], [keep, shift(give, "c", NC, 1)], [(F32, (2 * part, 2 * B))] * NY, []
    )
    sums = [sums[0]] + [shift(sums[u], "y", NY, u) for u in range(1, NY)]
    total, *chunks = call(
        sum_kernel,
        [pos],
        sums,
        [(F32, (2 * part, 2 * B))] + [(F32, (CHUNK, 2 * B))] * NX,
        [],
    )
    chunks = [chunks[0]] + [shift(chunks[u], "x", NX, u) for u in range(1, NX)]

    (few,) = call(select_few_kernel, [pos, panel_order], chunks, [(F32, (CHUNK, S))], [])
    near = lax.ppermute(few, "z", [(i, i ^ 1) for i in range(NZ)])
    (few,) = call(add_two_kernel, [], [few, near], [(F32, (CHUNK, S))], [])
    strip, rows, hots = call(
        select_kernel,
        where,
        [target_row, spread, rows],
        [(F32, (NZ, CHUNK, S)), (F32, (ROWS, 2 * B)), (BF16, (ROWS, S))],
        [],
    )
    far = [shift(few, "z", NZ, i) for i in (2, 4, 6)]
    far, strip = lax.optimization_barrier((far, strip))
    (few,) = call(add_four_kernel, [], [few, *far], [(F32, (CHUNK, S))], [])
    few, strip = lax.optimization_barrier((few, strip))
    strips = lax.all_to_all(strip, "z", 0, 0)
    few = gather(few, "x", NX)
    part1 = shift(strips, "x", NX, 1)
    part3 = shift(strips, "x", NX, 3)
    few = jnp.concatenate([few.reshape(NX * CHUNK, S), total], axis=1)
    few = gather(few, "y", NY)
    few, part1, part3 = lax.optimization_barrier((few, part1, part3))
    few_other = shift(few, "c", NC, 1)
    half = NZ // 2
    parts = [strips, part1, shift(part1[:half], "x", NX, 1), shift(part3[half:], "x", NX, 3), part3]
    solved = call(
        corner_kernel,
        [pos, panel_order],
        [few, few_other],
        [(F32, (S, S)), (F32, (S, 2 * B)), (BF16, (S, 2 * B)), (BF16, (S, 2 * B))],
        [
            pltpu.VMEM((B, B), F32),
            pltpu.VMEM((B, 2 * B), F32),
            pltpu.VMEM((S, S), F32),
            pltpu.VMEM((S, 2 * B), F32),
            pltpu.SMEM((B,), jnp.int32),
        ],
    )
    (out,) = call(
        update_kernel,
        [pos, panel_order],
        [hots, rows, *parts, few, few_other, *solved],
        [(F32, (ROWS * 2, B))],
        [pltpu.VMEM((ROWS, 2 * B), F32), pltpu.VMEM((S, S), F32), pltpu.VMEM((S, 2 * B), F32)],
    )
    return out.reshape(matrix.shape)


def solution(mesh):
    fine = Mesh(mesh.devices.reshape(NZ, NX, NY, NC), ("z", "x", "y", "c"))
    spec = P(None, ("y", "c"), None, None, ("z", "x"), None)
    return jax.shard_map(
        body,
        mesh=fine,
        in_specs=(spec, P(), P(), P(), P()),
        out_specs=spec,
        check_vma=False,
    )
```

```python
import jax
import jax.numpy as jnp
from jax import lax
from jax.experimental import pallas as pl
from jax.experimental.pallas import tpu as pltpu
from jax.sharding import Mesh, PartitionSpec as P

B = 128
PANELS = 4
S = PANELS * B
BR = 8
N_PROW = 8
N_PCOL = 32
NZ, NX, NY, NC = 8, 4, 4, 2
ROWS = BR * B
CHUNK = ROWS // N_PCOL
VMEM_LIMIT = 40 * 1024 * 1024
HIGHEST = lax.Precision.HIGHEST
F32 = jnp.float32
BF16 = jnp.bfloat16


def iota(shape, dim):
    return lax.broadcasted_iota(jnp.int32, shape, dim)


def dot_full(a, b):
    return jnp.dot(a, b, precision=HIGHEST, preferred_element_type=F32)


def dot_bf16(a, b):
    return jnp.dot(a, b, preferred_element_type=F32)


def split2(v):
    high = v.astype(BF16)
    low = (v - high.astype(F32)).astype(BF16)
    return high, low


def split3(v):
    high = v.astype(BF16)
    rest = v - high.astype(F32)
    middle = rest.astype(BF16)
    low = (rest - middle.astype(F32)).astype(BF16)
    return high, middle, low


def dot3(a, b):
    return dot_bf16(a[0], b[0]) + (dot_bf16(a[0], b[1]) + dot_bf16(a[1], b[0]))


def kept(value, here, row_width, col_width, same_block, row_start):
    rows = iota(value.shape, 0) + row_start
    cols = iota(value.shape, 1)
    value = jnp.where(here & (rows < row_width) & (cols < col_width), value, 0.0)
    return jnp.where(same_block & (rows == cols) & (rows >= row_width), 1.0, value)


def own_rows_kernel(pos, order, width, pattern, target_col, target_row, raw, keep, give, rows):
    r = pos[0]
    q = pos[1]
    c = pos[4]
    y = lax.div(r, NC)
    for t in range(BR):
        block_row = t * N_PROW + r
        for s in range(2):
            block_col = s * N_PCOL + q
            rows[t * B : (t + 1) * B, s * B : (s + 1) * B] = kept(
                raw[pl.ds(t * 2 * B + s, B, stride=2), :],
                pattern[block_row, block_col] > 0,
                width[block_row],
                width[block_col],
                block_row == block_col,
                0,
            )
    part = S // N_PROW
    high, middle, low = split3(rows[...])
    lane = iota((B, ROWS), 1)
    row_id = ((lane // B) * N_PROW + r) * B + lane % B
    for i in range(0, S, B):
        hot = jnp.where(row_id == target_col[i : i + B, :], 1.0, 0.0).astype(BF16)
        picked = dot_bf16(hot, high) + (dot_bf16(hot, middle) + dot_bf16(hot, low))
        place = lax.rem(i // B - y + NY, NY)
        keep[place, :part, :] = jnp.where(c == 0, picked[:part], picked[part:])
        give[place, :part, :] = jnp.where(c == 0, picked[part:], picked[:part])
    for k in range(PANELS):
        p = order[k]
        here = (p % N_PROW) == r
        block = rows[pl.ds(pl.multiple_of((p // N_PROW) * B, B), B), :]
        block = jnp.where(here, block, 0.0)
        place = lax.rem(k - y + NY, NY)
        keep[place, part:, :] = jnp.where(c == 0, block[:part], block[part:])
        give[place, part:, :] = jnp.where(c == 0, block[part:], block[:part])
    for t in range(BR):
        here = slice(t * B, (t + 1) * B)
        taken = is_target(target_row, B, (t * N_PROW + r) * B)
        rows[here, :] = jnp.where(taken, 0.0, rows[here, :])


def is_target(target_row, count, start):
    hot = jnp.where(iota((count, S), 0) + start == target_row[...], 1.0, 0.0)
    return jnp.max(hot, axis=1, keepdims=True) > 0.0


def add_kernel(keep, received, *sums):
    for u in range(NY):
        sums[u][...] = keep[u] + received[u]


def sum_kernel(pos, part0, part1, part2, part3, total, *chunks):
    x = pos[3]
    total[...] = (part0[...] + part1[...]) + (part2[...] + part3[...])
    count = CHUNK // 2
    for u in range(NX):
        start = lax.rem(x + u, NX) * count
        chunks[u][:count, :] = total[pl.ds(pl.multiple_of(start, count), count), :]
        chunks[u][count:, :] = total[pl.ds(pl.multiple_of(S // N_PROW + start, count), count), :]


def select_kernel(pos, order, width, pattern, target_row, spread, out):
    r = pos[0]
    z = pos[2]
    x = pos[3]
    block_row = z * N_PROW + r
    taken = is_target(target_row, CHUNK, block_row * B + x * CHUNK)
    for k in range(PANELS):
        p = order[k]
        source = lax.rem(p, N_PCOL)
        value = jnp.where(
            p >= N_PCOL,
            spread[source, pl.ds(1, CHUNK, stride=2), :],
            spread[source, pl.ds(0, CHUNK, stride=2), :],
        )
        value = kept(
            value, pattern[block_row, p] > 0, width[block_row], width[p], block_row == p, x * CHUNK
        )
        value = jnp.where(taken, 0.0, value)
        for j in range(NZ):
            out[j, :, k * B : (k + 1) * B] = value


def select_few_kernel(pos, order, chunk0, chunk1, chunk2, chunk3, out):
    z = pos[2]
    x = pos[3]
    for k in range(PANELS):
        p = order[k]
        source = lax.rem(p, N_PCOL)
        value = jnp.zeros((CHUNK, B), F32)
        for u, chunk in enumerate((chunk0, chunk1, chunk2, chunk3)):
            here = source == z * NX + lax.rem(x - u + NX, NX)
            value = jnp.where(here & (p < N_PCOL), chunk[:, :B], value)
            value = jnp.where(here & (p >= N_PCOL), chunk[:, B:], value)
        out[:, k * B : (k + 1) * B] = value


def add_two_kernel(a, b, out):
    out[...] = a[...] + b[...]


def add_four_kernel(a, b, c, d, out):
    out[...] = (a[...] + b[...]) + (c[...] + d[...])


def panel_order_rows(pos, same_core, other_core, first, out):
    c = pos[4]
    x = pos[3]
    y = lax.div(pos[0], NC)
    count = CHUNK // 2
    for u in range(NY):
        other_y = lax.rem(y - u + NY, NY)
        for core, group in ((c, same_core), (1 - c, other_core)):
            for j in range(NX):
                other_x = lax.rem(x - j + NX, NX)
                start = pl.multiple_of(((other_y * NC + core) * NX + other_x) * count, count)
                rows = slice(j * CHUNK + first, j * CHUNK + first + count)
                out[pl.ds(start, count), :] = group[u, rows, :S]


def own_order_rows(pos, same_core, other_core, first, out):
    c = pos[4]
    y = lax.div(pos[0], NC)
    part = S // N_PROW
    for u in range(NY):
        other_y = lax.rem(y - u + NY, NY)
        for core, group in ((c, same_core), (1 - c, other_core)):
            start = pl.multiple_of((other_y * NC + core) * part, part)
            out[pl.ds(start, part), :] = group[u, first : first + part, S:]


def panels_here(pos, order):
    found = [jnp.int32(-1), jnp.int32(-1)]
    for s in range(2):
        for k in range(PANELS):
            found[s] = jnp.where(order[k] == s * N_PCOL + pos[1], k, found[s])
    return found


def quick_invert(corner):
    row = iota((B, B), 0)
    col = iota((B, B), 1)
    eye = jnp.where(row == col, 1.0, 0.0)
    diagonal = jnp.where(row == col, corner, 0.0)
    by_col = 1.0 / jnp.sum(diagonal, axis=0, keepdims=True)
    by_row = 1.0 / jnp.sum(diagonal, axis=1, keepdims=True)
    corner_parts = split2(corner)
    approx = by_row * (eye + (eye - corner * by_col))
    high, low = split2(approx)
    residual = eye - dot3(corner_parts, (high, low))
    approx = approx + dot_bf16(high, residual.astype(BF16))
    residual = eye - dot_full(corner, approx)
    error = jnp.sum(residual * residual)
    return approx + dot_bf16(approx.astype(BF16), residual.astype(BF16)), error


def invert(corner, work, pivot_rows, out):
    row = iota((B, B), 0)
    col = iota((B, B), 1)
    eye = jnp.where(row == col, 1.0, 0.0)
    diagonal = jnp.where(row == col, corner, 0.0)
    by_col = 1.0 / jnp.sum(diagonal, axis=0, keepdims=True)
    by_row = 1.0 / jnp.sum(diagonal, axis=1, keepdims=True)
    residual = eye - corner * by_col
    approx = by_row * (eye + residual)

    def sweep(state):
        count, error, approx = state
        residual = eye - dot_full(corner, approx)
        return count + 1, jnp.max(jnp.abs(residual)), approx + dot_full(approx, residual)

    def again(state):
        count, error, approx = state
        return (count < 16) & jnp.logical_not(error < 1e-5)

    count, error, approx = lax.while_loop(again, sweep, (0, jnp.float32(1.0), approx))
    out[...] = approx

    @pl.when(jnp.logical_not(error < 1e-5))
    def _():
        work[:, :B] = corner
        work[:, B:] = eye
        row1 = iota((B, 1), 0)
        lane = iota((1, 2 * B), 1)

        def step(i, used):
            column = jnp.sum(jnp.where(iota((B, 2 * B), 1) == i, work[...], 0.0), axis=1, keepdims=True)
            size = jnp.where(used > 0.0, -1.0, jnp.abs(column))
            biggest = jnp.max(size)
            at = jnp.min(jnp.where(size == biggest, row1, B - 1))
            pivot_rows[i] = at
            line = jnp.sum(jnp.where(row1 == at, work[...], 0.0), axis=0, keepdims=True)
            line = line / jnp.sum(jnp.where(lane == i, line, 0.0))
            work[...] = jnp.where(row1 == at, line, work[...] - column * line)
            return jnp.where(row1 == at, 1.0, used)

        lax.fori_loop(0, B, step, jnp.zeros((B, 1), F32))

        def place(i, carry):
            line = jnp.sum(jnp.where(row1 == pivot_rows[i], work[:, B:], 0.0), axis=0, keepdims=True)
            out[...] = jnp.where(row1 == i, line, out[...])
            return carry

        lax.fori_loop(0, B, place, 0)


def corner_kernel(
    pos, order, few, few_other,
    factor, upper, steps_high, steps_low, inverses, work, solver, steps, pivot_rows,
):
    def eliminate(invert_block):
        panel_order_rows(pos, few, few_other, 0, factor)
        own_order_rows(pos, few, few_other, 0, upper)
        solver[...] = jnp.zeros((S, S), F32)
        error = jnp.float32(0.0)
        for k in range(PANELS):
            here = slice(k * B, (k + 1) * B)
            later = slice((k + 1) * B, S)
            before = slice(0, k * B)
            inverse, found = invert_block(factor[here, here])
            error = error + found
            inverse_parts = split2(inverse)
            solver[here, here] = inverse
            if k + 1 < PANELS:
                lower = dot3(split2(factor[later, here]), inverse_parts)
                factor[later, here] = lower
                lower_parts = split2(lower)
                factor[later, later] = factor[later, later] - dot3(lower_parts, split2(factor[here, later]))
                upper[later, :] = upper[later, :] - dot3(lower_parts, split2(upper[here, :]))
            if k:
                above = dot3(split2(solver[before, before]), split2(factor[before, here]))
                solver[before, here] = -dot3(split2(above), inverse_parts)
        return error

    def robust(corner):
        invert(corner, work, pivot_rows, inverses)
        return inverses[...], jnp.float32(0.0)

    error = eliminate(quick_invert)

    @pl.when(jnp.logical_not(error < 1e-6))
    def _():
        eliminate(robust)

    steps[...] = dot3(split2(solver[...]), split2(upper[...]))
    found = panels_here(pos, order)
    for s in range(2):

        @pl.when(found[s] >= 0)
        def _():
            steps[:, s * B : (s + 1) * B] = -solver[:, pl.ds(pl.multiple_of(found[s] * B, B), B)]

    high, low = split2(steps[...])
    steps_high[...] = high
    steps_low[...] = low


def update_kernel(
    pos, order, target_row, rows, part0, part1, part2a, part2b, part3, few, few_other,
    factor, upper, steps_high, steps_low,
    out, taken, home_rows, homes,
):
    r = pos[0]
    x = pos[3]
    half = S // 2
    steps_parts = (steps_high[...], steps_low[...])
    found = panels_here(pos, order)
    panel_order_rows(pos, few, few_other, CHUNK // 2, home_rows)
    own_order_rows(pos, few, few_other, S // N_PROW, homes)

    for i in range(2):
        here = slice(i * half, (i + 1) * half)
        product = dot3(split2(home_rows[here, :]), steps_parts)
        for s in range(2):
            cols = slice(s * B, (s + 1) * B)
            homes[here, cols] = jnp.where(found[s] >= 0, 0.0, homes[here, cols]) - product[:, cols]
    part2 = jnp.concatenate([part2a[...], part2b[...]], axis=0)
    for u, part in enumerate((part0[...], part1[...], part2, part3[...])):
        product = dot3(split2(part.reshape(NZ * CHUNK, S)), steps_parts)
        other_x = lax.rem(x - u + NX, NX)
        for i in range(NZ):
            place = pl.ds(pl.multiple_of(i * B + other_x * CHUNK, CHUNK), CHUNK)
            taken[place, :] = product[i * CHUNK : (i + 1) * CHUNK]

    home_parts = split3(homes[...])
    for t in range(BR):
        block_row = t * N_PROW + r
        here = slice(t * B, (t + 1) * B)
        hot = (iota((B, S), 0) + block_row * B) == target_row[...]
        hot = jnp.where(hot, 1.0, 0.0).astype(BF16)
        moved = dot_bf16(hot, home_parts[0]) + (dot_bf16(hot, home_parts[1]) + dot_bf16(hot, home_parts[2]))
        for s in range(2):
            cols = slice(s * B, (s + 1) * B)
            value = jnp.where(found[s] >= 0, 0.0, rows[here, cols])
            out[pl.ds(t * 2 * B + s, B, stride=2), :] = (value - taken[here, cols]) + moved[:, cols]

    for k in range(PANELS):

        @pl.when(lax.rem(order[k], N_PROW) == r)
        def _():
            t = lax.div(order[k], N_PROW)
            here = slice(k * B, (k + 1) * B)
            for s in range(2):
                at = pl.multiple_of(jnp.maximum(found[s], 0) * B, B)
                value = jnp.where(
                    found[s] >= 0, factor[here, pl.ds(at, B)], upper[here, s * B : (s + 1) * B]
                )
                out[pl.ds(t * 2 * B + s, B, stride=2), :] = value


def call(kernel, smem, vmem, out_shapes, scratch):
    in_specs = [pl.BlockSpec(memory_space=pltpu.SMEM)] * len(smem)
    in_specs += [pl.BlockSpec(memory_space=pltpu.VMEM)] * len(vmem)
    return pl.pallas_call(
        kernel,
        out_shape=[jax.ShapeDtypeStruct(shape, kind) for kind, shape in out_shapes],
        in_specs=in_specs,
        out_specs=[pl.BlockSpec(memory_space=pltpu.VMEM)] * len(out_shapes),
        scratch_shapes=scratch,
        compiler_params=pltpu.CompilerParams(vmem_limit_bytes=VMEM_LIMIT),
    )(*smem, *vmem)


def shift(value, axis, size, by):
    return lax.ppermute(value, axis, [(i, (i + by) % size) for i in range(size)])


def gather(value, axis, size):
    return jnp.stack([value] + [shift(value, axis, size, i) for i in range(1, size)])


def body(matrix, node_width, block_pattern, pivot_row_targets, panel_order):
    z = lax.axis_index("z")
    x = lax.axis_index("x")
    c = lax.axis_index("c")
    r = lax.axis_index("y") * NC + c
    pos = jnp.stack([r, z * NX + x, z, x, c]).astype(jnp.int32)
    raw = matrix.reshape(ROWS * 2, B)
    target_col = pivot_row_targets.reshape(S, 1)
    target_row = pivot_row_targets.reshape(1, S)
    where = [pos, panel_order, node_width, block_pattern]
    part = S // N_PROW

    spread = lax.all_to_all(raw.reshape(N_PCOL, CHUNK * 2, B), ("z", "x"), 0, 0)
    keep, give, rows = call(
        own_rows_kernel,
        where,
        [target_col, target_row, raw],
        [(F32, (NY, 2 * part, 2 * B)), (F32, (NY, 2 * part, 2 * B)), (F32, (ROWS, 2 * B))],
        [],
    )
    sums = call(
        add_kernel, [], [keep, shift(give, "c", NC, 1)], [(F32, (2 * part, 2 * B))] * NY, []
    )
    sums = [sums[0]] + [shift(sums[u], "y", NY, u) for u in range(1, NY)]
    total, *chunks = call(
        sum_kernel,
        [pos],
        sums,
        [(F32, (2 * part, 2 * B))] + [(F32, (CHUNK, 2 * B))] * NX,
        [],
    )
    chunks = [chunks[0]] + [shift(chunks[u], "x", NX, u) for u in range(1, NX)]

    (few,) = call(select_few_kernel, [pos, panel_order], chunks, [(F32, (CHUNK, S))], [])
    near = lax.ppermute(few, "z", [(i, i ^ 1) for i in range(NZ)])
    (few,) = call(add_two_kernel, [], [few, near], [(F32, (CHUNK, S))], [])
    (strip,) = call(select_kernel, where, [target_row, spread], [(F32, (NZ, CHUNK, S))], [])
    far = [shift(few, "z", NZ, i) for i in (2, 4, 6)]
    far, strip = lax.optimization_barrier((far, strip))
    (few,) = call(add_four_kernel, [], [few, *far], [(F32, (CHUNK, S))], [])
    few, strip = lax.optimization_barrier((few, strip))
    strips = lax.all_to_all(strip, "z", 0, 0)
    few = gather(few, "x", NX)
    part1 = shift(strips, "x", NX, 1)
    part3 = shift(strips, "x", NX, 3)
    few = jnp.concatenate([few.reshape(NX * CHUNK, S), total], axis=1)
    few = gather(few, "y", NY)
    few, part1, part3 = lax.optimization_barrier((few, part1, part3))
    few_other = shift(few, "c", NC, 1)
    half = NZ // 2
    parts = [strips, part1, shift(part1[:half], "x", NX, 1), shift(part3[half:], "x", NX, 3), part3]
    solved = call(
        corner_kernel,
        [pos, panel_order],
        [few, few_other],
        [(F32, (S, S)), (F32, (S, 2 * B)), (BF16, (S, 2 * B)), (BF16, (S, 2 * B))],
        [
            pltpu.VMEM((B, B), F32),
            pltpu.VMEM((B, 2 * B), F32),
            pltpu.VMEM((S, S), F32),
            pltpu.VMEM((S, 2 * B), F32),
            pltpu.SMEM((B,), jnp.int32),
        ],
    )
    (out,) = call(
        update_kernel,
        [pos, panel_order],
        [target_row, rows, *parts, few, few_other, *solved],
        [(F32, (ROWS * 2, B))],
        [pltpu.VMEM((ROWS, 2 * B), F32), pltpu.VMEM((S, S), F32), pltpu.VMEM((S, 2 * B), F32)],
    )
    return out.reshape(matrix.shape)


def solution(mesh):
    fine = Mesh(mesh.devices.reshape(NZ, NX, NY, NC), ("z", "x", "y", "c"))
    spec = P(None, ("y", "c"), None, None, ("z", "x"), None)
    return jax.shard_map(
        body,
        mesh=fine,
        in_specs=(spec, P(), P(), P(), P()),
        out_specs=spec,
        check_vma=False,
    )
```
